128 devices in a mesh: group: 16 (over z, y_hi, core), tp: 8 (over y_lo, x).
Axes of the slice: x: 4, y: 4 (y_hi: 2, y_lo: 2; y = y_hi * 2 + y_lo), z: 4, core: 2. Of those that a mesh axis runs over, the one named last changes fastest.
Arguments:
- q_prefill: bfloat16 [16384, 8192], P('group', 'tp'), may hold values from -6 to 62
- kv_fresh: bfloat16 [2, 16384, 1024], P(None, 'group', 'tp'), may hold values from -6 to 42
- kv_pool: bfloat16 [2, 3328, 64, 1024], P(None, 'group', None, 'tp'), may hold values from -6 to 42
- block_table: int32 [208, 16], P('group'), may hold values from 0 to 207, as said below
- lengths: int32 [208], replicated, may hold values from 1 to 1024, as said below
- owners: int32 [192], replicated, may hold values from 0 to 15, as said below
- q_decode: bfloat16 [1024, 4, 8192], P('group', None, 'tp'), may hold values from -6 to 62
- kv_steps: bfloat16 [2, 1024, 4, 1024], P(None, 'group', None, 'tp'), may hold values from -6 to 42
- kv_resident: bfloat16 [2, 512, 2048, 256], P(None, 'group', 'tp'), may hold values from -6 to 42
- resident_len: int32 [512], P('group'), may hold values from 1 to 512, as said below
Outputs:
- prefill_out: bfloat16 [16384, 8192], P('group', 'tp')
- decode_out: bfloat16 [1024, 4, 8192], P('group', None, 'tp')
The draws below stay inside these ranges and needn't reach their ends.
Inputs may be any that keep to these rules, and one draw needn't show every extreme that they name: `block_table`: each group's 12 + 1 rows (the last one for the prompt being prefilled) use each of that group's 208 blocks, numbered within the group, exactly once. In every group one of its 13 lengths is exactly 1024. `owners`: at most 2 of one group's finished requests go to one decode group; one decode group receives exactly 2 from every group. `resident_len`: in every group one request has exactly 512.
All inputs are finite; a program needn't handle non-finite values.
Results may differ from the reference program's by a relative error of at most 0.006.
Values may be sent and summed in bfloat16 or wider, within the bound.
A program may use at most 192 MiB of HBM per device.

```python
import jax
import jax.numpy as jnp
from jax import lax

KV_HEADS = 8
Q_PER_KV = 8
HEAD_DIM = 128
SEGMENT = 1024
MAXLEN = 1024
BLOCK = 64
RESIDENT = 32
RES_LEN = 512
STEPS = 4
CAPACITY = 2
GROUPS = 16
FINISHED = 12
NEW_ROWS = 32
DEC_ROWS = 64
PAIRS = 4
PAIR_HEADS = 2
POOL_BLOCKS = 208
TABLES = 208
PREFILL_TOKENS = 16384


def drawn_normal(key, shape):
    return jax.random.truncated_normal(key, -6.0, 6.0, shape, jnp.float32)


def draw_q_prefill(key, part):
    key = jax.random.fold_in(key, 11)
    shape = (PREFILL_TOKENS, KV_HEADS * Q_PER_KV * HEAD_DIM)
    return drawn_normal(key, shape).astype(jnp.bfloat16)


def draw_q_decode(key, part):
    key = jax.random.fold_in(key, 12)
    shape = (GROUPS * DEC_ROWS, STEPS, KV_HEADS * Q_PER_KV * HEAD_DIM)
    return drawn_normal(key, shape).astype(jnp.bfloat16)


def draw_kv_fresh(key, part):
    key = jax.random.fold_in(key, 13)
    shape = (2, PREFILL_TOKENS, KV_HEADS * HEAD_DIM)
    return drawn_normal(key, shape).astype(jnp.bfloat16)


def draw_kv_pool(key, part):
    key = jax.random.fold_in(key, 14)
    shape = (2, GROUPS * POOL_BLOCKS, BLOCK, KV_HEADS * HEAD_DIM)
    return drawn_normal(key, shape).astype(jnp.bfloat16)


def draw_kv_steps(key, part):
    key = jax.random.fold_in(key, 15)
    shape = (2, GROUPS * DEC_ROWS, STEPS, KV_HEADS * HEAD_DIM)
    return drawn_normal(key, shape).astype(jnp.bfloat16)


def draw_kv_resident(key, part):
    key = jax.random.fold_in(key, 16)
    shape = (2, GROUPS * RESIDENT, PAIRS * RES_LEN, PAIR_HEADS * HEAD_DIM)
    return drawn_normal(key, shape).astype(jnp.bfloat16)


def draw_block_table(key, part):
    key = jax.random.fold_in(key, 21)
    group_keys = jax.random.split(key, GROUPS)
    orders = jax.vmap(lambda one_key: jax.random.permutation(one_key, POOL_BLOCKS))(group_keys)
    return orders.reshape(TABLES, MAXLEN // BLOCK).astype(jnp.int32)


def draw_lengths(key, part):
    key = jax.random.fold_in(key, 22)
    first_key, second_key = jax.random.split(key)
    raw_lengths = jax.random.randint(first_key, (GROUPS, FINISHED + 1), 1, MAXLEN + 1)
    longest = jax.random.randint(second_key, (GROUPS, 1), 0, FINISHED + 1)
    column = lax.broadcasted_iota(jnp.int32, (GROUPS, FINISHED + 1), 1)
    return jnp.where(column == longest, MAXLEN, raw_lengths).reshape(TABLES).astype(jnp.int32)


def draw_owners(key, part):
    key = jax.random.fold_in(key, 23)
    first_key, second_key, third_key = jax.random.split(key, 3)
    busiest = jax.random.randint(first_key, (), 0, GROUPS)
    others = jax.vmap(lambda one_key: jax.random.permutation(one_key, GROUPS - 1))(jax.random.split(second_key, GROUPS))
    mapped = (busiest + 1 + others) % GROUPS
    base_list = jnp.concatenate([jnp.full((GROUPS, 2), busiest, jnp.int32), mapped[:, :FINISHED - 2].astype(jnp.int32)], axis=1)
    orders = jax.vmap(lambda one_key: jax.random.permutation(one_key, FINISHED))(jax.random.split(third_key, GROUPS))
    return jnp.take_along_axis(base_list, orders, axis=1).reshape(GROUPS * FINISHED).astype(jnp.int32)


def draw_resident_len(key, part):
    key = jax.random.fold_in(key, 24)
    first_key, second_key = jax.random.split(key)
    raw_lengths = jax.random.randint(first_key, (GROUPS, RESIDENT), 1, RES_LEN + 1)
    longest = jax.random.randint(second_key, (GROUPS, 1), 0, RESIDENT)
    column = lax.broadcasted_iota(jnp.int32, (GROUPS, RESIDENT), 1)
    return jnp.where(column == longest, RES_LEN, raw_lengths).reshape(GROUPS * RESIDENT).astype(jnp.int32)


def setup_inputs(seed: int = 0) -> dict:
    splits = jax.random.split(jax.random.key(seed), 11)
    return {
        "q_prefill": draw_q_prefill(jax.random.fold_in(splits[10], 71), 0),
        "kv_fresh": draw_kv_fresh(jax.random.fold_in(splits[10], 71), 0),
        "kv_pool": draw_kv_pool(jax.random.fold_in(splits[10], 71), 0),
        "block_table": draw_block_table(jax.random.fold_in(splits[10], 71), 0),
        "lengths": draw_lengths(jax.random.fold_in(splits[10], 71), 0),
        "owners": draw_owners(jax.random.fold_in(splits[10], 71), 0),
        "q_decode": draw_q_decode(jax.random.fold_in(splits[10], 71), 0),
        "kv_steps": draw_kv_steps(jax.random.fold_in(splits[10], 71), 0),
        "kv_resident": draw_kv_resident(jax.random.fold_in(splits[10], 71), 0),
        "resident_len": draw_resident_len(jax.random.fold_in(splits[10], 71), 0),
    }


NEG_FILL = -1e30


def soft_weights(scores):
    row_max = jnp.max(scores, axis=-1, keepdims=True)
    expo_vals = jnp.exp(scores - row_max)
    normalizer = jnp.sum(expo_vals, axis=-1)
    rounded = lax.optimization_barrier(expo_vals.astype(jnp.bfloat16)).astype(jnp.float32)
    return rounded, normalizer


def prefill_group(q_rows, fresh_kv, ctx_kv, ctx_length):
    score_scale = HEAD_DIM ** -0.5
    joined = jnp.concatenate([ctx_kv, fresh_kv], axis=1).astype(jnp.float32)
    key_span = joined.shape[1]
    joined = joined.reshape(2, key_span, KV_HEADS, HEAD_DIM).transpose(2, 0, 1, 3)
    queries = q_rows.astype(jnp.float32).reshape(SEGMENT, KV_HEADS, Q_PER_KV, HEAD_DIM).transpose(1, 2, 0, 3)
    position = lax.broadcasted_iota(jnp.int32, (SEGMENT, key_span), 1)
    token_idx = lax.broadcasted_iota(jnp.int32, (SEGMENT, key_span), 0)
    usable = jnp.where(position < MAXLEN, position < ctx_length, position - MAXLEN <= token_idx)

    def one_head(head_item):
        query_rows, kv_pair = head_item
        scores = jnp.einsum("qid,ld->qil", query_rows, kv_pair[0], precision=lax.Precision.HIGHEST) * score_scale
        scores = jnp.where(usable[None], scores, NEG_FILL)
        rounded, normalizer = soft_weights(scores)
        weighted = jnp.einsum("qil,ld->qid", rounded, kv_pair[1], precision=lax.Precision.HIGHEST)
        return (weighted / normalizer[..., None]).astype(jnp.bfloat16)

    head_outs = lax.map(one_head, (queries, joined))
    return head_outs.transpose(2, 0, 1, 3).reshape(SEGMENT, KV_HEADS * Q_PER_KV * HEAD_DIM)


def decode_rows(q_rows, kv_cache, length_vec, step_kv):
    score_scale = HEAD_DIM ** -0.5
    row_count, key_span = kv_cache.shape[1], kv_cache.shape[2]
    queries = q_rows.astype(jnp.float32).reshape(row_count, STEPS, KV_HEADS, Q_PER_KV, HEAD_DIM)
    cache_wide = kv_cache.astype(jnp.float32).reshape(2, row_count, key_span, KV_HEADS, HEAD_DIM)
    steps_wide = step_kv.astype(jnp.float32).reshape(2, row_count, STEPS, KV_HEADS, HEAD_DIM)
    cache_scores = jnp.einsum("rshqd,rlhd->rshql", queries, cache_wide[0], precision=lax.Precision.HIGHEST) * score_scale
    usable = jnp.arange(key_span, dtype=jnp.int32)[None, :] < length_vec[:, None]
    cache_scores = jnp.where(usable[:, None, None, None, :], cache_scores, NEG_FILL)
    step_scores = jnp.einsum("rshqd,rthd->rshqt", queries, steps_wide[0], precision=lax.Precision.HIGHEST) * score_scale
    step_index = lax.broadcasted_iota(jnp.int32, (STEPS, STEPS), 0)
    key_step = lax.broadcasted_iota(jnp.int32, (STEPS, STEPS), 1)
    causal = key_step <= step_index
    step_scores = jnp.where(causal[None, :, None, None, :], step_scores, NEG_FILL)
    scores = jnp.concatenate([cache_scores, step_scores], axis=-1)
    rounded, normalizer = soft_weights(scores)
    values = jnp.concatenate([cache_wide[1], steps_wide[1]], axis=1)
    weighted = jnp.einsum("rshql,rlhd->rshqd", rounded, values, precision=lax.Precision.HIGHEST)
    return (weighted / normalizer[..., None]).astype(jnp.bfloat16).reshape(row_count, STEPS, KV_HEADS * Q_PER_KV * HEAD_DIM)


def reference(q_prefill, kv_fresh, kv_pool, block_table, lengths, owners, q_decode, kv_steps, kv_resident, resident_len):
    group_ids = jnp.arange(GROUPS, dtype=jnp.int32)
    table_stride = FINISHED + 1

    def prefill_one(group_id):
        ctx_row = group_id * table_stride + FINISHED
        blocks = block_table[ctx_row] + group_id * POOL_BLOCKS
        ctx_kv = kv_pool[:, blocks].reshape(2, MAXLEN, KV_HEADS * HEAD_DIM)
        q_rows = lax.dynamic_slice_in_dim(q_prefill, (group_id * SEGMENT).astype(jnp.int32), SEGMENT, 0)
        fresh_kv = lax.dynamic_slice_in_dim(kv_fresh, (group_id * SEGMENT).astype(jnp.int32), SEGMENT, 1)
        return prefill_group(q_rows, fresh_kv, ctx_kv, lengths[ctx_row])

    prefill_out = lax.map(prefill_one, group_ids).reshape(PREFILL_TOKENS, KV_HEADS * Q_PER_KV * HEAD_DIM)

    owner_table = owners.reshape(GROUPS, FINISHED)
    same_owner = owner_table[:, :, None] == owner_table[:, None, :]
    earlier = lax.broadcasted_iota(jnp.int32, (FINISHED, FINISHED), 1) < lax.broadcasted_iota(jnp.int32, (FINISHED, FINISHED), 0)
    arrival_rank = jnp.sum((same_owner & earlier[None]).astype(jnp.int32), axis=2).astype(jnp.int32)
    slot_table = group_ids[:, None] * CAPACITY + arrival_rank
    table_rows = group_ids[:, None] * table_stride + jnp.arange(FINISHED, dtype=jnp.int32)[None, :]
    fin_lengths = lengths[table_rows]

    def decode_one(group_id):
        slot_ids = jnp.arange(NEW_ROWS, dtype=jnp.int32)
        matches = (owner_table == group_id)[None] & (slot_table[None] == slot_ids[:, None, None])
        chosen_row = jnp.sum(jnp.where(matches, table_rows[None], 0), axis=(1, 2)).astype(jnp.int32)
        new_length = jnp.sum(jnp.where(matches, fin_lengths[None], 0), axis=(1, 2)).astype(jnp.int32)
        blocks = block_table[chosen_row] + (chosen_row // table_stride)[:, None] * POOL_BLOCKS
        handed = kv_pool[:, blocks].reshape(2, NEW_ROWS, MAXLEN, KV_HEADS * HEAD_DIM)
        resident = lax.dynamic_slice_in_dim(kv_resident, (group_id * RESIDENT).astype(jnp.int32), RESIDENT, 1)
        resident = resident.reshape(2, RESIDENT, PAIRS, RES_LEN, PAIR_HEADS, HEAD_DIM).transpose(0, 1, 3, 2, 4, 5)
        resident = resident.reshape(2, RESIDENT, RES_LEN, KV_HEADS * HEAD_DIM)
        res_length = lax.dynamic_slice_in_dim(resident_len, (group_id * RESIDENT).astype(jnp.int32), RESIDENT, 0)
        q_rows = lax.dynamic_slice_in_dim(q_decode, (group_id * DEC_ROWS).astype(jnp.int32), DEC_ROWS, 0)
        step_kv = lax.dynamic_slice_in_dim(kv_steps, (group_id * DEC_ROWS).astype(jnp.int32), DEC_ROWS, 1)
        resident_out = decode_rows(q_rows[:RESIDENT], resident, res_length, step_kv[:, :RESIDENT])
        arrival_out = decode_rows(q_rows[RESIDENT:], handed, new_length, step_kv[:, RESIDENT:])
        return jnp.concatenate([resident_out, arrival_out], axis=0)

    decode_out = lax.map(decode_one, group_ids).reshape(GROUPS * DEC_ROWS, STEPS, KV_HEADS * Q_PER_KV * HEAD_DIM)
    return prefill_out, decode_out
```

```python
import functools

import jax
import jax.numpy as jnp
from jax import lax
from jax.experimental import pallas as pl
from jax.experimental.pallas import tpu as pltpu
from jax.sharding import PartitionSpec as P

HEAD_DIM = 128
Q_PER_KV = 8
MAXLEN = 1024
CAPACITY = 2
NEG_FILL = -1e30
SCALE = HEAD_DIM ** -0.5 * 1.4426950408889634
PACK = 96
TILE = 128
STACK = 4
MESH = pl.DeviceIdType.MESH
BF16 = jnp.bfloat16
F32 = jnp.float32


def dot_nt(a, b):
    return lax.dot_general(a, b, (((1,), (1,)), ((), ())), preferred_element_type=F32)


def dot_nn(a, b):
    return jnp.dot(a, b, preferred_element_type=F32)


def heads_to_rows(x):
    wide = x.astype(F32)
    parts = [wide[:, a * HEAD_DIM:(a + 1) * HEAD_DIM] for a in range(Q_PER_KV)]
    return jnp.concatenate(parts, axis=0).astype(BF16)


def kernel(
    groups,
    qp_hbm,
    fresh_hbm,
    pool_hbm,
    table,
    lengths,
    owners,
    qd_hbm,
    steps_hbm,
    res_hbm,
    res_len,
    pout_hbm,
    dout_hbm,
    qp,
    fresh,
    pool,
    qd,
    steps,
    res,
    pout,
    dout,
    kbuf,
    vbuf,
    diag,
    q_own,
    q_partner,
    pack_send,
    pack_recv,
    ks_res,
    ks_arr,
    step_only,
    ans,
    ans_send,
    ans_recv,
    part_send,
    part_recv,
    stat_send,
    stat_recv,
    own_part,
    own_stat,
    load_sem,
    out_sem,
    pack_send_sem,
    pack_recv_sem,
    ans_send_sem,
    ans_recv_sem,
    pair_send_sem,
    pair_recv_sem,
):
    me = lax.axis_index("group")
    tp = lax.axis_index("tp")
    side = tp % 2
    partner = tp + 1 - 2 * side
    finished = owners.shape[0] // groups
    res_rows = res.shape[1]
    span_res = res.shape[2]
    n_step = qd.shape[1]
    q_rows = Q_PER_KV * n_step
    seg = qp.shape[0]

    barrier = pltpu.get_barrier_semaphore()

    def greet(d, carry):
        pl.semaphore_signal(
            barrier, inc=1, device_id={"group": (me + d) % groups}, device_id_type=MESH
        )
        return carry

    lax.fori_loop(1, groups, greet, 0)
    pl.semaphore_signal(barrier, inc=1, device_id={"tp": partner}, device_id_type=MESH)

    loads = [
        pltpu.make_async_copy(qd_hbm, qd, load_sem.at[0]),
        pltpu.make_async_copy(steps_hbm, steps, load_sem.at[1]),
        pltpu.make_async_copy(fresh_hbm, fresh, load_sem.at[2]),
        pltpu.make_async_copy(pool_hbm, pool, load_sem.at[3]),
        pltpu.make_async_copy(qp_hbm, qp, load_sem.at[4]),
        pltpu.make_async_copy(res_hbm, res, load_sem.at[5]),
    ]
    for one in loads:
        one.start()

    loads[0].wait()
    loads[1].wait()

    def relay_res(r, carry):
        q_own[r] = heads_to_rows(qd[r])
        return carry

    lax.fori_loop(0, res_rows, relay_res, 0, unroll=4)

    def relay_arr(o, carry):
        first = res_rows + o * CAPACITY
        for c in range(CAPACITY):
            pack_send[o, c * q_rows:(c + 1) * q_rows] = heads_to_rows(qd[first + c])
        for k in range(2):
            rows = [steps[k, first + c].astype(F32) for c in range(CAPACITY)]
            rows.append(jnp.zeros((16 - CAPACITY * n_step, HEAD_DIM), F32))
            start = CAPACITY * q_rows + 16 * k
            pack_send[o, start:start + 16] = jnp.concatenate(rows, axis=0).astype(BF16)
        return carry

    lax.fori_loop(0, groups, relay_arr, 0, unroll=2)

    pl.semaphore_wait(barrier, groups)

    def pack_copy(peer):
        return pltpu.make_async_remote_copy(
            src_ref=pack_send.at[peer],
            dst_ref=pack_recv.at[me],
            send_sem=pack_send_sem.at[peer],
            recv_sem=pack_recv_sem.at[me],
            device_id={"group": peer},
            device_id_type=MESH,
        )

    def pair_copy(src, dst, i):
        return pltpu.make_async_remote_copy(
            src_ref=src,
            dst_ref=dst,
            send_sem=pair_send_sem.at[i],
            recv_sem=pair_recv_sem.at[i],
            device_id={"tp": partner},
            device_id_type=MESH,
        )

    q_pair = pair_copy(q_own, q_partner, 0)
    q_pair.start()

    def send_pack(d, carry):
        pack_copy((me + d) % groups).start()
        return carry

    lax.fori_loop(1, groups, send_pack, 0)
    pack_recv[me] = pack_send[me]

    per_tile = 16 // n_step

    def gather_steps(i, carry):
        for k in range(2):
            for base, dst in ((0, ks_res), (res_rows, ks_arr)):
                rows = [steps[k, base + i * per_tile + c].astype(F32) for c in range(per_tile)]
                dst[k, pl.ds(pl.multiple_of(i * 16, 16), 16)] = jnp.concatenate(
                    rows, axis=0
                ).astype(BF16)
        return carry

    lax.fori_loop(0, res_rows // per_tile, gather_steps, 0, unroll=2)

    loads[2].wait()
    loads[3].wait()
    ctx_len = lengths[me * (finished + 1) + finished]
    first_key = pool[0, table[finished, 0]][0:1]
    block = pool.shape[2]
    for b in range(MAXLEN // block):
        blk = table[finished, b]
        valid = lax.broadcasted_iota(jnp.int32, (block, HEAD_DIM), 0) + b * block < ctx_len
        kbuf[b * block:(b + 1) * block] = jnp.where(
            valid, pool[0, blk].astype(F32), first_key.astype(F32)
        ).astype(BF16)
        vbuf[b * block:(b + 1) * block, :HEAD_DIM] = jnp.where(
            valid, pool[1, blk].astype(F32), 0.0
        ).astype(BF16)
        vbuf[b * block:(b + 1) * block, HEAD_DIM:] = jnp.where(valid, 1.0, 0.0).astype(BF16)
    kbuf[MAXLEN:] = fresh[0]
    vbuf[MAXLEN:, :HEAD_DIM] = fresh[1]
    vbuf[MAXLEN:, HEAD_DIM:] = jnp.ones((seg, HEAD_DIM), BF16)
    row = lax.broadcasted_iota(jnp.int32, (STACK * TILE, TILE), 0) % TILE
    col = lax.broadcasted_iota(jnp.int32, (STACK * TILE, TILE), 1)
    diag[...] = jnp.where(col <= row, 0.0, NEG_FILL)
    loads[4].wait()

    def prefill(first_head):
        cols = [slice((first_head + h) * HEAD_DIM, (first_head + h + 1) * HEAD_DIM) for h in range(STACK)]
        for i in range(seg // TILE):
            rows = slice(i * TILE, (i + 1) * TILE)
            span = MAXLEN + (i + 1) * TILE
            q = jnp.concatenate([qp[rows, c] for c in cols], axis=0)
            s = dot_nt(q, kbuf[:span])
            s = jnp.concatenate([s[:, :span - TILE], s[:, span - TILE:] + diag[...]], axis=1)
            top = jnp.max(s, axis=1, keepdims=True)
            p = jnp.exp2(s * SCALE - top * SCALE).astype(BF16)
            o = dot_nn(p, vbuf[:span])
            o = (o[:, :HEAD_DIM] / o[:, HEAD_DIM:]).astype(BF16)
            for h in range(STACK):
                pout[rows, cols[h]] = o[h * TILE:(h + 1) * TILE]

    prefill(0)
    half = STACK * HEAD_DIM
    out_first = pltpu.make_async_copy(
        pout.at[:, pl.ds(0, half)], pout_hbm.at[:, pl.ds(0, half)], out_sem.at[0]
    )
    out_first.start()

    loads[5].wait()
    q_pair.wait()
    lane = lax.broadcasted_iota(jnp.int32, (q_rows, HEAD_DIM), 1)
    position = side * span_res + lax.broadcasted_iota(jnp.int32, (q_rows, span_res), 1)

    def partner_rows(r, carry):
        tops, norms = carry
        cols = pl.ds(pl.multiple_of((1 - side) * HEAD_DIM, HEAD_DIM), HEAD_DIM)
        s = dot_nt(q_partner[r], res[0, r, :, cols])
        s = jnp.where(position < res_len[r], s * SCALE, NEG_FILL)
        top = jnp.max(s, axis=1, keepdims=True)
        p = jnp.exp2(s - top)
        norm = jnp.sum(p, axis=1, keepdims=True)
        part_send[r] = dot_nn(p.astype(BF16), res[1, r, :, cols]).astype(BF16)
        return jnp.where(lane == r, top, tops), jnp.where(lane == r, norm, norms)

    zeros = jnp.zeros((q_rows, HEAD_DIM), F32)
    tops, norms = lax.fori_loop(0, res_rows, partner_rows, (zeros, zeros), unroll=4)
    stat_send[0] = tops
    stat_send[1] = norms
    part_pair = pair_copy(part_send, part_recv, 1)
    part_pair.start()
    stat_pair = pair_copy(stat_send, stat_recv, 2)
    stat_pair.start()

    def wait_pack(d, carry):
        peer = (me + d) % groups
        pltpu.make_async_remote_copy(
            src_ref=pack_send.at[peer],
            dst_ref=pack_recv.at[peer],
            send_sem=pack_send_sem.at[peer],
            recv_sem=pack_recv_sem.at[peer],
            device_id={"group": peer},
            device_id_type=MESH,
        ).wait()
        return carry

    lax.fori_loop(1, groups, wait_pack, 0)

    owner_of = [owners[me * finished + f] for f in range(finished)]
    slot_of = []
    for f in range(finished):
        rank = jnp.int32(0)
        for f2 in range(f):
            rank = rank + jnp.where(owner_of[f2] == owner_of[f], 1, 0)
        slot_of.append(owner_of[f] * CAPACITY + rank)

    cache_pos = lax.broadcasted_iota(jnp.int32, (q_rows, MAXLEN), 1)
    step_row = lax.broadcasted_iota(jnp.int32, (q_rows, 16), 0) % n_step
    step_col = lax.broadcasted_iota(jnp.int32, (q_rows, 16), 1)

    def finished_row(f):
        length = lengths[me * (finished + 1) + f]
        owner = owner_of[f]
        rank = slot_of[f] - owner * CAPACITY
        q = jnp.where(
            rank == 0,
            pack_recv[owner, 0:q_rows].astype(F32),
            pack_recv[owner, q_rows:2 * q_rows].astype(F32),
        ).astype(BF16)
        step_k = pack_recv[owner, 2 * q_rows:2 * q_rows + 16]
        step_v = pack_recv[owner, 2 * q_rows + 16:2 * q_rows + 32]
        blks = [table[f, b] for b in range(MAXLEN // block)]
        keys = jnp.concatenate([pool[0, b] for b in blks], axis=0)
        values = jnp.concatenate([pool[1, b] for b in blks], axis=0)
        s = jnp.where(cache_pos < length, dot_nt(q, keys) * SCALE, NEG_FILL)
        seen = (step_col // n_step == rank) & (step_col % n_step <= step_row)
        s2 = jnp.where(seen, dot_nt(q, step_k) * SCALE, NEG_FILL)
        top = jnp.maximum(jnp.max(s, axis=1, keepdims=True), jnp.max(s2, axis=1, keepdims=True))
        p = jnp.exp2(s - top)
        p2 = jnp.exp2(s2 - top)
        norm = jnp.sum(p, axis=1, keepdims=True) + jnp.sum(p2, axis=1, keepdims=True)
        o = dot_nn(p.astype(BF16), values) + dot_nn(p2.astype(BF16), step_v)
        ans[f] = (o / norm).astype(BF16)

    for f in range(finished):
        finished_row(f)

    for n in range(groups * CAPACITY):
        f = jnp.int32(0)
        for j in range(1, finished):
            f = f + jnp.where(slot_of[j] == n, j, 0)
        ans_send[n // CAPACITY, (n % CAPACITY) * q_rows:(n % CAPACITY + 1) * q_rows] = ans[f]

    def send_answer(d, carry):
        peer = (me + d) % groups
        pltpu.make_async_remote_copy(
            src_ref=ans_send.at[peer],
            dst_ref=ans_recv.at[me],
            send_sem=ans_send_sem.at[peer],
            recv_sem=ans_recv_sem.at[me],
            device_id={"group": peer},
            device_id_type=MESH,
        ).start()
        return carry

    lax.fori_loop(1, groups, send_answer, 0)
    ans_recv[me] = ans_send[me]

    q_all = pack_send[:, :CAPACITY * q_rows].reshape(groups * CAPACITY * q_rows, HEAD_DIM)
    n_rows, n_cols = groups * CAPACITY * q_rows, groups * CAPACITY * n_step
    r_id = lax.broadcasted_iota(jnp.int32, (n_rows, n_cols), 0)
    c_id = lax.broadcasted_iota(jnp.int32, (n_rows, n_cols), 1)
    seen_all = (r_id // q_rows == c_id // n_step) & (c_id % n_step <= r_id % n_step)
    s = jnp.where(seen_all, dot_nt(q_all, ks_arr[0]) * SCALE, NEG_FILL)
    p = jnp.exp2(s - jnp.max(s, axis=1, keepdims=True))
    o = dot_nn(p.astype(BF16), ks_arr[1]) / jnp.sum(p, axis=1, keepdims=True)
    step_only[...] = o.astype(BF16).reshape(groups, CAPACITY * q_rows, HEAD_DIM)

    row_id = lax.broadcasted_iota(jnp.int32, (q_rows, res_rows * n_step), 0)
    col_id = lax.broadcasted_iota(jnp.int32, (q_rows, res_rows * n_step), 1)

    def own_rows(r, carry):
        tops, norms = carry
        cols = pl.ds(pl.multiple_of(side * HEAD_DIM, HEAD_DIM), HEAD_DIM)
        q = q_own[r]
        s = dot_nt(q, res[0, r, :, cols])
        s = jnp.where(position < res_len[r], s * SCALE, NEG_FILL)
        seen = (col_id // n_step == r) & (col_id % n_step <= row_id % n_step)
        s2 = jnp.where(seen, dot_nt(q, ks_res[0]) * SCALE, NEG_FILL)
        top = jnp.maximum(jnp.max(s, axis=1, keepdims=True), jnp.max(s2, axis=1, keepdims=True))
        p = jnp.exp2(s - top)
        p2 = jnp.exp2(s2 - top)
        norm = jnp.sum(p, axis=1, keepdims=True) + jnp.sum(p2, axis=1, keepdims=True)
        own_part[r] = dot_nn(p.astype(BF16), res[1, r, :, cols]) + dot_nn(p2.astype(BF16), ks_res[1])
        return jnp.where(lane == r, top, tops), jnp.where(lane == r, norm, norms)

    tops, norms = lax.fori_loop(0, res_rows, own_rows, (zeros, zeros), unroll=4)
    own_stat[0] = tops
    own_stat[1] = norms

    prefill(STACK)
    out_second = pltpu.make_async_copy(
        pout.at[:, pl.ds(half, half)], pout_hbm.at[:, pl.ds(half, half)], out_sem.at[1]
    )
    out_second.start()

    part_pair.wait()
    stat_pair.wait()

    def put_row(dst_row, x):
        for a in range(Q_PER_KV):
            dout[dst_row, :, a * HEAD_DIM:(a + 1) * HEAD_DIM] = x[a * n_step:(a + 1) * n_step].astype(BF16)

    joint = jnp.maximum(own_stat[0], stat_recv[0])
    scale_own = jnp.exp2(own_stat[0] - joint)
    scale_got = jnp.exp2(stat_recv[0] - joint)
    inverse = 1.0 / (own_stat[1] * scale_own + stat_recv[1] * scale_got)
    own_stat[0] = scale_own * inverse
    own_stat[1] = scale_got * inverse

    def merge(r, carry):
        w_own = jnp.sum(jnp.where(lane == r, own_stat[0], 0.0), axis=1, keepdims=True)
        w_got = jnp.sum(jnp.where(lane == r, own_stat[1], 0.0), axis=1, keepdims=True)
        put_row(r, own_part[r] * w_own + part_recv[r].astype(F32) * w_got)
        return carry

    lax.fori_loop(0, res_rows, merge, 0, unroll=4)

    def wait_answer(d, carry):
        peer = (me + d) % groups
        pltpu.make_async_remote_copy(
            src_ref=ans_send.at[peer],
            dst_ref=ans_recv.at[peer],
            send_sem=ans_send_sem.at[peer],
            recv_sem=ans_recv_sem.at[peer],
            device_id={"group": peer},
            device_id_type=MESH,
        ).wait()
        return carry

    lax.fori_loop(1, groups, wait_answer, 0)

    def arrive(src, carry):
        count = jnp.int32(0)
        for f in range(finished):
            count = count + jnp.where(owners[src * finished + f] == me, 1, 0)
        for c in range(CAPACITY):
            rows = slice(c * q_rows, (c + 1) * q_rows)
            x = jnp.where(
                count > c, ans_recv[src, rows].astype(F32), step_only[src, rows].astype(F32)
            )
            put_row(res_rows + src * CAPACITY + c, x)
        return carry

    lax.fori_loop(0, groups, arrive, 0, unroll=2)
    out_dec = pltpu.make_async_copy(dout, dout_hbm, out_sem.at[2])
    out_dec.start()
    out_first.wait()
    out_second.wait()
    out_dec.wait()


def per_device(*args):
    q_prefill, kv_fresh, kv_pool, table, lengths, owners, q_decode, kv_steps, kv_res, res_len = args
    groups = lax.axis_size("group")
    rows, n_step, width = q_decode.shape
    res_rows = kv_res.shape[1]
    arr_rows = rows - res_rows
    q_rows = Q_PER_KV * n_step
    seg = q_prefill.shape[0]
    finished = owners.shape[0] // groups
    vmem = pltpu.VMEM
    scratch = [
        vmem(q_prefill.shape, BF16),
        vmem(kv_fresh.shape, BF16),
        vmem(kv_pool.shape, BF16),
        vmem(q_decode.shape, BF16),
        vmem(kv_steps.shape, BF16),
        vmem(kv_res.shape, BF16),
        vmem(q_prefill.shape, BF16),
        vmem(q_decode.shape, BF16),
        vmem((MAXLEN + seg, HEAD_DIM), BF16),
        vmem((MAXLEN + seg, 2 * HEAD_DIM), BF16),
        vmem((STACK * TILE, TILE), F32),
        vmem((res_rows, q_rows, HEAD_DIM), BF16),
        vmem((res_rows, q_rows, HEAD_DIM), BF16),
        vmem((groups, PACK, HEAD_DIM), BF16),
        vmem((groups, PACK, HEAD_DIM), BF16),
        vmem((2, res_rows * n_step, HEAD_DIM), BF16),
        vmem((2, arr_rows * n_step, HEAD_DIM), BF16),
        vmem((groups, CAPACITY * q_rows, HEAD_DIM), BF16),
        vmem((finished, q_rows, HEAD_DIM), BF16),
        vmem((groups, CAPACITY * q_rows, HEAD_DIM), BF16),
        vmem((groups, CAPACITY * q_rows, HEAD_DIM), BF16),
        vmem((res_rows, q_rows, HEAD_DIM), BF16),
        vmem((res_rows, q_rows, HEAD_DIM), BF16),
        vmem((2, q_rows, HEAD_DIM), F32),
        vmem((2, q_rows, HEAD_DIM), F32),
        vmem((res_rows, q_rows, HEAD_DIM), F32),
        vmem((2, q_rows, HEAD_DIM), F32),
        pltpu.SemaphoreType.DMA((6,)),
        pltpu.SemaphoreType.DMA((3,)),
        pltpu.SemaphoreType.DMA((groups,)),
        pltpu.SemaphoreType.DMA((groups,)),
        pltpu.SemaphoreType.DMA((groups,)),
        pltpu.SemaphoreType.DMA((groups,)),
        pltpu.SemaphoreType.DMA((3,)),
        pltpu.SemaphoreType.DMA((3,)),
    ]
    hbm = pl.BlockSpec(memory_space=pl.ANY)
    smem = pl.BlockSpec(memory_space=pltpu.SMEM)
    return pl.pallas_call(
        functools.partial(kernel, groups),
        out_shape=(
            jax.ShapeDtypeStruct(q_prefill.shape, BF16),
            jax.ShapeDtypeStruct(q_decode.shape, BF16),
        ),
        in_specs=[hbm, hbm, hbm, smem, smem, smem, hbm, hbm, hbm, smem],
        out_specs=(hbm, hbm),
        scratch_shapes=scratch,
        compiler_params=pltpu.CompilerParams(
            collective_id=0, has_side_effects=True, vmem_limit_bytes=56 * 2**20
        ),
        cost_estimate=pl.CostEstimate(
            flops=8 * 10**9, bytes_accessed=21 * 10**6, transcendentals=14 * 10**6
        ),
    )(*args)


def solution(mesh):
    in_specs = (
        P("group", "tp"),
        P(None, "group", "tp"),
        P(None, "group", None, "tp"),
        P("group", None),
        P(),
        P(),
        P("group", None, "tp"),
        P(None, "group", None, "tp"),
        P(None, "group", "tp", None),
        P("group"),
    )
    out_specs = (P("group", "tp"), P("group", None, "tp"))
    return jax.shard_map(
        per_device, mesh=mesh, in_specs=in_specs, out_specs=out_specs, check_vma=False
    )
```

```python
import functools

import jax
import jax.numpy as jnp
from jax import lax
from jax.experimental import pallas as pl
from jax.experimental.pallas import tpu as pltpu
from jax.sharding import PartitionSpec as P

HEAD_DIM = 128
Q_PER_KV = 8
MAXLEN = 1024
CAPACITY = 2
NEG_FILL = -1e30
SCALE = HEAD_DIM ** -0.5 * 1.4426950408889634
PACK = 96
TILE = 128
STACK = 8
BATCH = 8
FIN_BATCH = 4
MESH = pl.DeviceIdType.MESH
BF16 = jnp.bfloat16
F32 = jnp.float32


def dot_nt(a, b):
    return lax.dot_general(a, b, (((1,), (1,)), ((), ())), preferred_element_type=F32)


def dot_nn(a, b):
    return jnp.dot(a, b, preferred_element_type=F32)


def heads_to_rows(x):
    wide = x.astype(F32)
    parts = [wide[:, a * HEAD_DIM:(a + 1) * HEAD_DIM] for a in range(Q_PER_KV)]
    return jnp.concatenate(parts, axis=0).astype(BF16)


def kernel(
    groups,
    qp_hbm,
    fresh_hbm,
    pool_hbm,
    table,
    lengths,
    owners,
    qd_hbm,
    steps_hbm,
    res_hbm,
    res_len,
    pout_hbm,
    dout_hbm,
    qp,
    fresh,
    pool,
    qd,
    steps,
    res,
    pout,
    dout,
    kbuf,
    vbuf,
    diag,
    q_pair,
    pack_send,
    pack_recv,
    ks_res,
    ks_arr,
    step_part,
    step_stat,
    step_only,
    ans,
    ans_send,
    ans_recv,
    part_send,
    part_recv,
    stat_send,
    stat_recv,
    own_part,
    own_stat,
    load_sem,
    out_sem,
    pack_send_sem,
    pack_recv_sem,
    ans_send_sem,
    ans_recv_sem,
    pair_send_sem,
    pair_recv_sem,
):
    me = lax.axis_index("group")
    tp = lax.axis_index("tp")
    side = tp % 2
    partner = tp + 1 - 2 * side
    finished = owners.shape[0] // groups
    res_rows = res.shape[1]
    span_res = res.shape[2]
    n_step = qd.shape[1]
    q_rows = Q_PER_KV * n_step
    seg = qp.shape[0]

    barrier = pltpu.get_barrier_semaphore()

    def greet(d, carry):
        pl.semaphore_signal(
            barrier, inc=1, device_id={"group": (me + d) % groups}, device_id_type=MESH
        )
        return carry

    lax.fori_loop(1, groups, greet, 0)
    pl.semaphore_signal(barrier, inc=1, device_id={"tp": partner}, device_id_type=MESH)

    loads = [
        pltpu.make_async_copy(qd_hbm, qd, load_sem.at[0]),
        pltpu.make_async_copy(steps_hbm, steps, load_sem.at[1]),
        pltpu.make_async_copy(fresh_hbm, fresh, load_sem.at[2]),
        pltpu.make_async_copy(pool_hbm, pool, load_sem.at[3]),
        pltpu.make_async_copy(qp_hbm, qp, load_sem.at[4]),
        pltpu.make_async_copy(res_hbm, res, load_sem.at[5]),
    ]
    for one in loads:
        one.start()

    loads[0].wait()
    loads[1].wait()

    def relay_res(r, carry):
        q_pair[side, r] = heads_to_rows(qd[r])
        return carry

    lax.fori_loop(0, res_rows, relay_res, 0, unroll=4)

    def relay_arr(o, carry):
        first = res_rows + o * CAPACITY
        for c in range(CAPACITY):
            pack_send[o, c * q_rows:(c + 1) * q_rows] = heads_to_rows(qd[first + c])
        for k in range(2):
            rows = [steps[k, first + c].astype(F32) for c in range(CAPACITY)]
            rows.append(jnp.zeros((16 - CAPACITY * n_step, HEAD_DIM), F32))
            start = CAPACITY * q_rows + 16 * k
            pack_send[o, start:start + 16] = jnp.concatenate(rows, axis=0).astype(BF16)
        return carry

    lax.fori_loop(0, groups, relay_arr, 0, unroll=2)

    per_tile = 16 // n_step

    def gather_steps(i, carry):
        for k in range(2):
            for base, dst in ((0, ks_res), (res_rows, ks_arr)):
                rows = [steps[k, base + i * per_tile + c].astype(F32) for c in range(per_tile)]
                dst[k, pl.ds(pl.multiple_of(i * 16, 16), 16)] = jnp.concatenate(
                    rows, axis=0
                ).astype(BF16)
        return carry

    lax.fori_loop(0, res_rows // per_tile, gather_steps, 0, unroll=2)

    loads[2].wait()
    loads[3].wait()
    ctx_len = lengths[me * (finished + 1) + finished]
    first_key = pool[0, table[finished, 0]][0:1]
    block = pool.shape[2]
    for b in range(MAXLEN // block):
        blk = table[finished, b]
        valid = lax.broadcasted_iota(jnp.int32, (block, HEAD_DIM), 0) + b * block < ctx_len
        kbuf[b * block:(b + 1) * block] = jnp.where(
            valid, pool[0, blk].astype(F32), first_key.astype(F32)
        ).astype(BF16)
        vbuf[b * block:(b + 1) * block, :HEAD_DIM] = jnp.where(
            valid, pool[1, blk].astype(F32), 0.0
        ).astype(BF16)
        vbuf[b * block:(b + 1) * block, HEAD_DIM:] = jnp.where(valid, 1.0, 0.0).astype(BF16)
    kbuf[MAXLEN:] = fresh[0]
    vbuf[MAXLEN:, :HEAD_DIM] = fresh[1]
    vbuf[MAXLEN:, HEAD_DIM:] = jnp.ones((seg, HEAD_DIM), BF16)
    row = lax.broadcasted_iota(jnp.int32, (STACK * TILE, TILE), 0) % TILE
    col = lax.broadcasted_iota(jnp.int32, (STACK * TILE, TILE), 1)
    diag[...] = jnp.where(col <= row, 0.0, NEG_FILL)
    loads[4].wait()

    def prefill(i):
        rows = slice(i * TILE, (i + 1) * TILE)
        span = MAXLEN + (i + 1) * TILE
        cols = [slice(h * HEAD_DIM, (h + 1) * HEAD_DIM) for h in range(STACK)]
        q = jnp.concatenate([qp[rows, c] for c in cols], axis=0)
        s = dot_nt(q, kbuf[:span])
        s = jnp.concatenate([s[:, :span - TILE], s[:, span - TILE:] + diag[...]], axis=1)
        top = jnp.max(s, axis=1, keepdims=True)
        p = jnp.exp2(s * SCALE - top * SCALE).astype(BF16)
        o = dot_nn(p, vbuf[:span])
        o = (o[:, :HEAD_DIM] / o[:, HEAD_DIM:]).astype(BF16)
        for h in range(STACK):
            pout[rows, cols[h]] = o[h * TILE:(h + 1) * TILE]

    def out_rows(first, last, i):
        rows = pl.ds(first * TILE, (last - first) * TILE)
        copy = pltpu.make_async_copy(pout.at[rows], pout_hbm.at[rows], out_sem.at[i])
        copy.start()
        return copy

    prefill(0)

    pl.semaphore_wait(barrier, groups)

    def pack_copy(peer):
        return pltpu.make_async_remote_copy(
            src_ref=pack_send.at[peer],
            dst_ref=pack_recv.at[me],
            send_sem=pack_send_sem.at[peer],
            recv_sem=pack_recv_sem.at[me],
            device_id={"group": peer},
            device_id_type=MESH,
        )

    def pair_copy(src, dst, i):
        return pltpu.make_async_remote_copy(
            src_ref=src,
            dst_ref=dst,
            send_sem=pair_send_sem.at[i],
            recv_sem=pair_recv_sem.at[i],
            device_id={"tp": partner},
            device_id_type=MESH,
        )

    q_copy = pair_copy(q_pair.at[side], q_pair.at[side], 0)
    q_copy.start()

    def send_pack(d, carry):
        pack_copy((me + d) % groups).start()
        return carry

    lax.fori_loop(1, groups, send_pack, 0)
    pack_recv[me] = pack_send[me]


    for i in range(1, 5):
        prefill(i)
    out_first = out_rows(0, 5, 0)

    loads[5].wait()
    q_copy.wait()
    lane = lax.broadcasted_iota(jnp.int32, (q_rows, HEAD_DIM), 1)
    position = side * span_res + lax.broadcasted_iota(jnp.int32, (2 * q_rows, span_res), 1)
    empty = jnp.zeros((q_rows, HEAD_DIM), BF16)

    def resident_rows(i, carry):
        tops, norms = carry
        rows = [i * BATCH + b for b in range(BATCH)]
        scores = []
        for r in rows:
            q = jnp.concatenate(
                [
                    jnp.concatenate([q_pair[0, r], empty], axis=1),
                    jnp.concatenate([empty, q_pair[1, r]], axis=1),
                ],
                axis=0,
            )
            scores.append(dot_nt(q, res[0, r]))
        scores = [
            jnp.where(position < res_len[r], s * SCALE, NEG_FILL) for r, s in zip(rows, scores)
        ]
        maxima = [jnp.max(s, axis=1, keepdims=True) for s in scores]
        weights = [jnp.exp2(s - m) for s, m in zip(scores, maxima)]
        sums = [jnp.sum(p, axis=1, keepdims=True) for p in weights]
        outs = [dot_nn(p.astype(BF16), res[1, r]) for r, p in zip(rows, weights)]
        for r, m, l, o in zip(rows, maxima, sums, outs):
            for u in range(2):
                head = slice(u * q_rows, (u + 1) * q_rows)
                part = o[head, u * HEAD_DIM:(u + 1) * HEAD_DIM]
                own_part[u, r] = part
                part_send[u, r] = part.astype(BF16)
                own_stat[0, u, r] = jnp.broadcast_to(m[head], (q_rows, HEAD_DIM))
                own_stat[1, u, r] = jnp.broadcast_to(l[head], (q_rows, HEAD_DIM))
            give = jnp.where(side == 0, m[q_rows:], m[:q_rows])
            tops = jnp.where(lane == r, give, tops)
            give = jnp.where(side == 0, l[q_rows:], l[:q_rows])
            norms = jnp.where(lane == r, give, norms)
        return tops, norms

    zeros = jnp.zeros((q_rows, HEAD_DIM), F32)
    tops, norms = lax.fori_loop(0, res_rows // BATCH, resident_rows, (zeros, zeros))
    stat_send[0] = tops
    stat_send[1] = norms
    part_pair = pair_copy(part_send.at[1 - side], part_recv, 1)
    part_pair.start()
    stat_pair = pair_copy(stat_send, stat_recv, 2)
    stat_pair.start()

    def wait_pack(d, carry):
        peer = (me + d) % groups
        pltpu.make_async_remote_copy(
            src_ref=pack_send.at[peer],
            dst_ref=pack_recv.at[peer],
            send_sem=pack_send_sem.at[peer],
            recv_sem=pack_recv_sem.at[peer],
            device_id={"group": peer},
            device_id_type=MESH,
        ).wait()
        return carry

    lax.fori_loop(1, groups, wait_pack, 0)

    owner_of = [owners[me * finished + f] for f in range(finished)]
    slot_of = []
    for f in range(finished):
        rank = jnp.int32(0)
        for f2 in range(f):
            rank = rank + jnp.where(owner_of[f2] == owner_of[f], 1, 0)
        slot_of.append(owner_of[f] * CAPACITY + rank)

    cache_pos = lax.broadcasted_iota(jnp.int32, (q_rows, MAXLEN), 1)
    step_row = lax.broadcasted_iota(jnp.int32, (q_rows, 16), 0) % n_step
    step_col = lax.broadcasted_iota(jnp.int32, (q_rows, 16), 1)

    def finished_rows(batch):
        scores, step_scores, step_values = [], [], []
        for f in batch:
            owner = owner_of[f]
            rank = slot_of[f] - owner * CAPACITY
            q = jnp.where(
                rank == 0,
                pack_recv[owner, 0:q_rows].astype(F32),
                pack_recv[owner, q_rows:2 * q_rows].astype(F32),
            ).astype(BF16)
            keys = jnp.concatenate([pool[0, table[f, b]] for b in range(MAXLEN // block)], axis=0)
            length = lengths[me * (finished + 1) + f]
            scores.append(jnp.where(cache_pos < length, dot_nt(q, keys) * SCALE, NEG_FILL))
            seen = (step_col // n_step == rank) & (step_col % n_step <= step_row)
            step_k = pack_recv[owner, 2 * q_rows:2 * q_rows + 16]
            step_scores.append(jnp.where(seen, dot_nt(q, step_k) * SCALE, NEG_FILL))
            step_values.append(pack_recv[owner, 2 * q_rows + 16:2 * q_rows + 32])
        maxima = [
            jnp.maximum(jnp.max(s, axis=1, keepdims=True), jnp.max(s2, axis=1, keepdims=True))
            for s, s2 in zip(scores, step_scores)
        ]
        weights = [jnp.exp2(s - m) for s, m in zip(scores, maxima)]
        step_weights = [jnp.exp2(s - m) for s, m in zip(step_scores, maxima)]
        sums = [
            jnp.sum(p, axis=1, keepdims=True) + jnp.sum(p2, axis=1, keepdims=True)
            for p, p2 in zip(weights, step_weights)
        ]
        for f, p, p2, v2, l in zip(batch, weights, step_weights, step_values, sums):
            values = jnp.concatenate([pool[1, table[f, b]] for b in range(MAXLEN // block)], axis=0)
            o = dot_nn(p.astype(BF16), values) + dot_nn(p2.astype(BF16), v2)
            ans[f] = (o / l).astype(BF16)

    for first in range(0, finished, FIN_BATCH):
        finished_rows(range(first, min(first + FIN_BATCH, finished)))

    for n in range(groups * CAPACITY):
        f = jnp.int32(0)
        for j in range(1, finished):
            f = f + jnp.where(slot_of[j] == n, j, 0)
        ans_send[n // CAPACITY, (n % CAPACITY) * q_rows:(n % CAPACITY + 1) * q_rows] = ans[f]

    def send_answer(d, carry):
        peer = (me + d) % groups
        pltpu.make_async_remote_copy(
            src_ref=ans_send.at[peer],
            dst_ref=ans_recv.at[me],
            send_sem=ans_send_sem.at[peer],
            recv_sem=ans_recv_sem.at[me],
            device_id={"group": peer},
            device_id_type=MESH,
        ).start()
        return carry

    lax.fori_loop(1, groups, send_answer, 0)
    ans_recv[me] = ans_send[me]


    n_rows, n_cols = res_rows * q_rows, res_rows * n_step
    r_id = lax.broadcasted_iota(jnp.int32, (n_rows, n_cols), 0)
    c_id = lax.broadcasted_iota(jnp.int32, (n_rows, n_cols), 1)
    seen_all = (r_id // q_rows == c_id // n_step) & (c_id % n_step <= r_id % n_step)

    def all_steps(q, keys, values):
        s = jnp.where(seen_all, dot_nt(q, keys) * SCALE, NEG_FILL)
        top = jnp.max(s, axis=1, keepdims=True)
        p = jnp.exp2(s - top)
        return dot_nn(p.astype(BF16), values), top, jnp.sum(p, axis=1, keepdims=True)

    q_arr = pack_send[:, :CAPACITY * q_rows].reshape(n_rows, HEAD_DIM)
    o, top, norm = all_steps(q_arr, ks_arr[0], ks_arr[1])
    step_only[...] = (o / norm).astype(BF16).reshape(groups, CAPACITY * q_rows, HEAD_DIM)
    q_res = q_pair[side].reshape(n_rows, HEAD_DIM)
    o, top, norm = all_steps(q_res, ks_res[0], ks_res[1])
    rows3 = (res_rows, q_rows, HEAD_DIM)
    step_part[...] = o.reshape(rows3)
    step_stat[0] = jnp.broadcast_to(top, o.shape).reshape(rows3)
    step_stat[1] = jnp.broadcast_to(norm, o.shape).reshape(rows3)

    for i in range(5, 8):
        prefill(i)
    out_second = out_rows(5, 8, 1)

    part_pair.wait()
    stat_pair.wait()

    def put_row(dst_row, x):
        for a in range(Q_PER_KV):
            dout[dst_row, :, a * HEAD_DIM:(a + 1) * HEAD_DIM] = x[a * n_step:(a + 1) * n_step].astype(BF16)

    def merge(r, carry):
        top_own, top_step = own_stat[0, side, r], step_stat[0, r]
        top_got = jnp.sum(jnp.where(lane == r, stat_recv[0], 0.0), axis=1, keepdims=True)
        norm_got = jnp.sum(jnp.where(lane == r, stat_recv[1], 0.0), axis=1, keepdims=True)
        joint = jnp.maximum(jnp.maximum(top_own, top_step), top_got)
        w_own = jnp.exp2(top_own - joint)
        w_step = jnp.exp2(top_step - joint)
        w_got = jnp.exp2(top_got - joint)
        norm = own_stat[1, side, r] * w_own + step_stat[1, r] * w_step + norm_got * w_got
        x = own_part[side, r] * w_own + step_part[r] * w_step + part_recv[r].astype(F32) * w_got
        put_row(r, x / norm)
        return carry

    lax.fori_loop(0, res_rows, merge, 0, unroll=4)

    def wait_answer(d, carry):
        peer = (me + d) % groups
        pltpu.make_async_remote_copy(
            src_ref=ans_send.at[peer],
            dst_ref=ans_recv.at[peer],
            send_sem=ans_send_sem.at[peer],
            recv_sem=ans_recv_sem.at[peer],
            device_id={"group": peer},
            device_id_type=MESH,
        ).wait()
        return carry

    lax.fori_loop(1, groups, wait_answer, 0)

    def arrive(src, carry):
        count = jnp.int32(0)
        for f in range(finished):
            count = count + jnp.where(owners[src * finished + f] == me, 1, 0)
        for c in range(CAPACITY):
            rows = slice(c * q_rows, (c + 1) * q_rows)
            x = jnp.where(
                count > c, ans_recv[src, rows].astype(F32), step_only[src, rows].astype(F32)
            )
            put_row(res_rows + src * CAPACITY + c, x)
        return carry

    lax.fori_loop(0, groups, arrive, 0, unroll=2)
    out_dec = pltpu.make_async_copy(dout, dout_hbm, out_sem.at[2])
    out_dec.start()
    out_first.wait()
    out_second.wait()
    out_dec.wait()


def per_device(*args):
    q_prefill, kv_fresh, kv_pool, table, lengths, owners, q_decode, kv_steps, kv_res, res_len = args
    groups = lax.axis_size("group")
    rows, n_step, width = q_decode.shape
    res_rows = kv_res.shape[1]
    arr_rows = rows - res_rows
    q_rows = Q_PER_KV * n_step
    seg = q_prefill.shape[0]
    finished = owners.shape[0] // groups
    vmem = pltpu.VMEM
    scratch = [
        vmem(q_prefill.shape, BF16),
        vmem(kv_fresh.shape, BF16),
        vmem(kv_pool.shape, BF16),
        vmem(q_decode.shape, BF16),
        vmem(kv_steps.shape, BF16),
        vmem(kv_res.shape, BF16),
        vmem(q_prefill.shape, BF16),
        vmem(q_decode.shape, BF16),
        vmem((MAXLEN + seg, HEAD_DIM), BF16),
        vmem((MAXLEN + seg, 2 * HEAD_DIM), BF16),
        vmem((STACK * TILE, TILE), F32),
        vmem((2, res_rows, q_rows, HEAD_DIM), BF16),
        vmem((groups, PACK, HEAD_DIM), BF16),
        vmem((groups, PACK, HEAD_DIM), BF16),
        vmem((2, res_rows * n_step, HEAD_DIM), BF16),
        vmem((2, arr_rows * n_step, HEAD_DIM), BF16),
        vmem((res_rows, q_rows, HEAD_DIM), F32),
        vmem((2, res_rows, q_rows, HEAD_DIM), F32),
        vmem((groups, CAPACITY * q_rows, HEAD_DIM), BF16),
        vmem((finished, q_rows, HEAD_DIM), BF16),
        vmem((groups, CAPACITY * q_rows, HEAD_DIM), BF16),
        vmem((groups, CAPACITY * q_rows, HEAD_DIM), BF16),
        vmem((2, res_rows, q_rows, HEAD_DIM), BF16),
        vmem((res_rows, q_rows, HEAD_DIM), BF16),
        vmem((2, q_rows, HEAD_DIM), F32),
        vmem((2, q_rows, HEAD_DIM), F32),
        vmem((2, res_rows, q_rows, HEAD_DIM), F32),
        vmem((2, 2, res_rows, q_rows, HEAD_DIM), F32),
        pltpu.SemaphoreType.DMA((6,)),
        pltpu.SemaphoreType.DMA((3,)),
        pltpu.SemaphoreType.DMA((groups,)),
        pltpu.SemaphoreType.DMA((groups,)),
        pltpu.SemaphoreType.DMA((groups,)),
        pltpu.SemaphoreType.DMA((groups,)),
        pltpu.SemaphoreType.DMA((3,)),
        pltpu.SemaphoreType.DMA((3,)),
    ]
    hbm = pl.BlockSpec(memory_space=pl.ANY)
    smem = pl.BlockSpec(memory_space=pltpu.SMEM)
    return pl.pallas_call(
        functools.partial(kernel, groups),
        out_shape=(
            jax.ShapeDtypeStruct(q_prefill.shape, BF16),
            jax.ShapeDtypeStruct(q_decode.shape, BF16),
        ),
        in_specs=[hbm, hbm, hbm, smem, smem, smem, hbm, hbm, hbm, smem],
        out_specs=(hbm, hbm),
        scratch_shapes=scratch,
        compiler_params=pltpu.CompilerParams(
            collective_id=0, has_side_effects=True, vmem_limit_bytes=56 * 2**20
        ),
        cost_estimate=pl.CostEstimate(
            flops=8 * 10**9, bytes_accessed=21 * 10**6, transcendentals=14 * 10**6
        ),
    )(*args)


def solution(mesh):
    in_specs = (
        P("group", "tp"),
        P(None, "group", "tp"),
        P(None, "group", None, "tp"),
        P("group", None),
        P(),
        P(),
        P("group", None, "tp"),
        P(None, "group", None, "tp"),
        P(None, "group", "tp", None),
        P("group"),
    )
    out_specs = (P("group", "tp"), P("group", None, "tp"))
    return jax.shard_map(
        per_device, mesh=mesh, in_specs=in_specs, out_specs=out_specs, check_vma=False
    )
```

```python
import functools

import jax
import jax.numpy as jnp
from jax import lax
from jax.experimental import pallas as pl
from jax.experimental.pallas import tpu as pltpu
from jax.sharding import PartitionSpec as P

HEAD_DIM = 128
Q_PER_KV = 8
MAXLEN = 1024
CAPACITY = 2
NEG_FILL = -1e30
SCALE = HEAD_DIM ** -0.5 * 1.4426950408889634
PACK = 96
TILE = 128
STACK = 8
BATCH = 8
FIN_BATCH = 4
MESH = pl.DeviceIdType.MESH
BF16 = jnp.bfloat16
F32 = jnp.float32


def dot_nt(a, b):
    return lax.dot_general(a, b, (((1,), (1,)), ((), ())), preferred_element_type=F32)


def dot_nn(a, b):
    return jnp.dot(a, b, preferred_element_type=F32)


def heads_to_rows(x):
    wide = x.astype(F32)
    parts = [wide[:, a * HEAD_DIM:(a + 1) * HEAD_DIM] for a in range(Q_PER_KV)]
    return jnp.concatenate(parts, axis=0).astype(BF16)


def kernel(
    groups,
    qp_hbm,
    fresh_hbm,
    pool_hbm,
    table,
    lengths,
    owners,
    qd_hbm,
    steps_hbm,
    res_hbm,
    res_len,
    pout_hbm,
    dout_hbm,
    qp,
    fresh,
    pool,
    qd,
    steps,
    res,
    pout,
    dout,
    kbuf,
    vbuf,
    diag,
    q_pair,
    pack_send,
    pack_recv,
    ks_res,
    ks_arr,
    step_part,
    step_stat,
    step_only,
    ans,
    ans_send,
    ans_recv,
    part_send,
    part_recv,
    stat_send,
    stat_recv,
    own_part,
    own_stat,
    load_sem,
    out_sem,
    pack_send_sem,
    pack_recv_sem,
    ans_send_sem,
    ans_recv_sem,
    pair_send_sem,
    pair_recv_sem,
):
    me = lax.axis_index("group")
    tp = lax.axis_index("tp")
    side = tp % 2
    partner = tp + 1 - 2 * side
    finished = owners.shape[0] // groups
    res_rows = res.shape[1]
    span_res = res.shape[2]
    n_step = qd.shape[1]
    q_rows = Q_PER_KV * n_step
    seg = qp.shape[0]

    barrier = pltpu.get_barrier_semaphore()

    def greet(d, carry):
        pl.semaphore_signal(
            barrier, inc=1, device_id={"group": (me + d) % groups}, device_id_type=MESH
        )
        return carry

    lax.fori_loop(1, groups, greet, 0)
    pl.semaphore_signal(barrier, inc=1, device_id={"tp": partner}, device_id_type=MESH)

    loads = [
        pltpu.make_async_copy(qd_hbm, qd, load_sem.at[0]),
        pltpu.make_async_copy(steps_hbm, steps, load_sem.at[1]),
        pltpu.make_async_copy(fresh_hbm, fresh, load_sem.at[2]),
        pltpu.make_async_copy(pool_hbm, pool, load_sem.at[3]),
        pltpu.make_async_copy(qp_hbm, qp, load_sem.at[4]),
        pltpu.make_async_copy(res_hbm, res, load_sem.at[5]),
    ]
    for one in loads[:5]:
        one.start()

    loads[0].wait()
    loads[1].wait()

    def relay_res(r, carry):
        q_pair[side, r] = heads_to_rows(qd[r])
        return carry

    lax.fori_loop(0, res_rows, relay_res, 0, unroll=4)

    def relay_arr(o, carry):
        first = res_rows + o * CAPACITY
        for c in range(CAPACITY):
            pack_send[o, c * q_rows:(c + 1) * q_rows] = heads_to_rows(qd[first + c])
        for k in range(2):
            rows = [steps[k, first + c].astype(F32) for c in range(CAPACITY)]
            rows.append(jnp.zeros((16 - CAPACITY * n_step, HEAD_DIM), F32))
            start = CAPACITY * q_rows + 16 * k
            pack_send[o, start:start + 16] = jnp.concatenate(rows, axis=0).astype(BF16)
        return carry

    lax.fori_loop(0, groups, relay_arr, 0, unroll=2)

    pl.semaphore_wait(barrier, groups)

    def pack_copy(peer):
        return pltpu.make_async_remote_copy(
            src_ref=pack_send.at[peer],
            dst_ref=pack_recv.at[me],
            send_sem=pack_send_sem.at[peer],
            recv_sem=pack_recv_sem.at[me],
            device_id={"group": peer},
            device_id_type=MESH,
        )

    def pair_copy(src, dst, i):
        return pltpu.make_async_remote_copy(
            src_ref=src,
            dst_ref=dst,
            send_sem=pair_send_sem.at[i],
            recv_sem=pair_recv_sem.at[i],
            device_id={"tp": partner},
            device_id_type=MESH,
        )

    q_copy = pair_copy(q_pair.at[side], q_pair.at[side], 0)
    q_copy.start()

    def send_pack(d, carry):
        pack_copy((me + d) % groups).start()
        return carry

    lax.fori_loop(1, groups, send_pack, 0)
    pack_recv[me] = pack_send[me]


    per_tile = 16 // n_step

    def gather_steps(i, carry):
        for k in range(2):
            for base, dst in ((0, ks_res), (res_rows, ks_arr)):
                rows = [steps[k, base + i * per_tile + c].astype(F32) for c in range(per_tile)]
                dst[k, pl.ds(pl.multiple_of(i * 16, 16), 16)] = jnp.concatenate(
                    rows, axis=0
                ).astype(BF16)
        return carry

    lax.fori_loop(0, res_rows // per_tile, gather_steps, 0, unroll=2)

    loads[2].wait()
    loads[3].wait()
    loads[5].start()
    ctx_len = lengths[me * (finished + 1) + finished]
    first_key = pool[0, table[finished, 0]][0:1]
    block = pool.shape[2]
    for b in range(MAXLEN // block):
        blk = table[finished, b]
        valid = lax.broadcasted_iota(jnp.int32, (block, HEAD_DIM), 0) + b * block < ctx_len
        kbuf[b * block:(b + 1) * block] = jnp.where(
            valid, pool[0, blk].astype(F32), first_key.astype(F32)
        ).astype(BF16)
        vbuf[b * block:(b + 1) * block, :HEAD_DIM] = jnp.where(
            valid, pool[1, blk].astype(F32), 0.0
        ).astype(BF16)
        vbuf[b * block:(b + 1) * block, HEAD_DIM:] = jnp.where(valid, 1.0, 0.0).astype(BF16)
    kbuf[MAXLEN:] = fresh[0]
    vbuf[MAXLEN:, :HEAD_DIM] = fresh[1]
    vbuf[MAXLEN:, HEAD_DIM:] = jnp.ones((seg, HEAD_DIM), BF16)
    row = lax.broadcasted_iota(jnp.int32, (STACK * TILE, TILE), 0) % TILE
    col = lax.broadcasted_iota(jnp.int32, (STACK * TILE, TILE), 1)
    diag[...] = jnp.where(col <= row, 0.0, NEG_FILL)
    loads[4].wait()

    def prefill(i):
        rows = slice(i * TILE, (i + 1) * TILE)
        span = MAXLEN + (i + 1) * TILE
        cols = [slice(h * HEAD_DIM, (h + 1) * HEAD_DIM) for h in range(STACK)]
        q = jnp.concatenate([qp[rows, c] for c in cols], axis=0)
        s = dot_nt(q, kbuf[:span])
        s = jnp.concatenate([s[:, :span - TILE], s[:, span - TILE:] + diag[...]], axis=1)
        top = jnp.max(s, axis=1, keepdims=True)
        p = jnp.exp2(s * SCALE - top * SCALE).astype(BF16)
        o = dot_nn(p, vbuf[:span])
        o = (o[:, :HEAD_DIM] / o[:, HEAD_DIM:]).astype(BF16)
        for h in range(STACK):
            pout[rows, cols[h]] = o[h * TILE:(h + 1) * TILE]

    def out_rows(first, last, i):
        rows = pl.ds(first * TILE, (last - first) * TILE)
        copy = pltpu.make_async_copy(pout.at[rows], pout_hbm.at[rows], out_sem.at[i])
        copy.start()
        return copy

    for i in range(5):
        prefill(i)
    out_first = out_rows(0, 5, 0)

    loads[5].wait()
    q_copy.wait()
    lane = lax.broadcasted_iota(jnp.int32, (q_rows, HEAD_DIM), 1)
    position = side * span_res + lax.broadcasted_iota(jnp.int32, (2 * q_rows, span_res), 1)
    empty = jnp.zeros((q_rows, HEAD_DIM), BF16)

    def resident_rows(i, carry):
        tops, norms = carry
        rows = [i * BATCH + b for b in range(BATCH)]
        scores = []
        for r in rows:
            q = jnp.concatenate(
                [
                    jnp.concatenate([q_pair[0, r], empty], axis=1),
                    jnp.concatenate([empty, q_pair[1, r]], axis=1),
                ],
                axis=0,
            )
            scores.append(dot_nt(q, res[0, r]))
        scores = [
            jnp.where(position < res_len[r], s * SCALE, NEG_FILL) for r, s in zip(rows, scores)
        ]
        maxima = [jnp.max(s, axis=1, keepdims=True) for s in scores]
        weights = [jnp.exp2(s - m) for s, m in zip(scores, maxima)]
        sums = [jnp.sum(p, axis=1, keepdims=True) for p in weights]
        outs = [dot_nn(p.astype(BF16), res[1, r]) for r, p in zip(rows, weights)]
        for r, m, l, o in zip(rows, maxima, sums, outs):
            for u in range(2):
                head = slice(u * q_rows, (u + 1) * q_rows)
                part = o[head, u * HEAD_DIM:(u + 1) * HEAD_DIM]
                own_part[u, r] = part
                part_send[u, r] = part.astype(BF16)
                own_stat[0, u, r] = jnp.broadcast_to(m[head], (q_rows, HEAD_DIM))
                own_stat[1, u, r] = jnp.broadcast_to(l[head], (q_rows, HEAD_DIM))
            give = jnp.where(side == 0, m[q_rows:], m[:q_rows])
            tops = jnp.where(lane == r, give, tops)
            give = jnp.where(side == 0, l[q_rows:], l[:q_rows])
            norms = jnp.where(lane == r, give, norms)
        return tops, norms

    zeros = jnp.zeros((q_rows, HEAD_DIM), F32)
    tops, norms = lax.fori_loop(0, res_rows // BATCH, resident_rows, (zeros, zeros))
    stat_send[0] = tops
    stat_send[1] = norms
    part_pair = pair_copy(part_send.at[1 - side], part_recv, 1)
    part_pair.start()
    stat_pair = pair_copy(stat_send, stat_recv, 2)
    stat_pair.start()

    def wait_pack(d, carry):
        peer = (me + d) % groups
        pltpu.make_async_remote_copy(
            src_ref=pack_send.at[peer],
            dst_ref=pack_recv.at[peer],
            send_sem=pack_send_sem.at[peer],
            recv_sem=pack_recv_sem.at[peer],
            device_id={"group": peer},
            device_id_type=MESH,
        ).wait()
        return carry

    lax.fori_loop(1, groups, wait_pack, 0)

    owner_of = [owners[me * finished + f] for f in range(finished)]
    slot_of = []
    for f in range(finished):
        rank = jnp.int32(0)
        for f2 in range(f):
            rank = rank + jnp.where(owner_of[f2] == owner_of[f], 1, 0)
        slot_of.append(owner_of[f] * CAPACITY + rank)

    cache_pos = lax.broadcasted_iota(jnp.int32, (q_rows, MAXLEN), 1)
    step_row = lax.broadcasted_iota(jnp.int32, (q_rows, 16), 0) % n_step
    step_col = lax.broadcasted_iota(jnp.int32, (q_rows, 16), 1)

    def finished_rows(batch):
        scores, step_scores, step_values = [], [], []
        for f in batch:
            owner = owner_of[f]
            rank = slot_of[f] - owner * CAPACITY
            q = jnp.where(
                rank == 0,
                pack_recv[owner, 0:q_rows].astype(F32),
                pack_recv[owner, q_rows:2 * q_rows].astype(F32),
            ).astype(BF16)
            keys = jnp.concatenate([pool[0, table[f, b]] for b in range(MAXLEN // block)], axis=0)
            length = lengths[me * (finished + 1) + f]
            scores.append(jnp.where(cache_pos < length, dot_nt(q, keys) * SCALE, NEG_FILL))
            seen = (step_col // n_step == rank) & (step_col % n_step <= step_row)
            step_k = pack_recv[owner, 2 * q_rows:2 * q_rows + 16]
            step_scores.append(jnp.where(seen, dot_nt(q, step_k) * SCALE, NEG_FILL))
            step_values.append(pack_recv[owner, 2 * q_rows + 16:2 * q_rows + 32])
        maxima = [
            jnp.maximum(jnp.max(s, axis=1, keepdims=True), jnp.max(s2, axis=1, keepdims=True))
            for s, s2 in zip(scores, step_scores)
        ]
        weights = [jnp.exp2(s - m) for s, m in zip(scores, maxima)]
        step_weights = [jnp.exp2(s - m) for s, m in zip(step_scores, maxima)]
        sums = [
            jnp.sum(p, axis=1, keepdims=True) + jnp.sum(p2, axis=1, keepdims=True)
            for p, p2 in zip(weights, step_weights)
        ]
        for f, p, p2, v2, l in zip(batch, weights, step_weights, step_values, sums):
            values = jnp.concatenate([pool[1, table[f, b]] for b in range(MAXLEN // block)], axis=0)
            o = dot_nn(p.astype(BF16), values) + dot_nn(p2.astype(BF16), v2)
            ans[f] = (o / l).astype(BF16)

    for first in range(0, finished, FIN_BATCH):
        finished_rows(range(first, min(first + FIN_BATCH, finished)))

    for n in range(groups * CAPACITY):
        f = jnp.int32(0)
        for j in range(1, finished):
            f = f + jnp.where(slot_of[j] == n, j, 0)
        ans_send[n // CAPACITY, (n % CAPACITY) * q_rows:(n % CAPACITY + 1) * q_rows] = ans[f]

    def send_answer(d, carry):
        peer = (me + d) % groups
        pltpu.make_async_remote_copy(
            src_ref=ans_send.at[peer],
            dst_ref=ans_recv.at[me],
            send_sem=ans_send_sem.at[peer],
            recv_sem=ans_recv_sem.at[me],
            device_id={"group": peer},
            device_id_type=MESH,
        ).start()
        return carry

    lax.fori_loop(1, groups, send_answer, 0)
    ans_recv[me] = ans_send[me]


    n_rows, n_cols = res_rows * q_rows, res_rows * n_step
    r_id = lax.broadcasted_iota(jnp.int32, (n_rows, n_cols), 0)
    c_id = lax.broadcasted_iota(jnp.int32, (n_rows, n_cols), 1)
    seen_all = (r_id // q_rows == c_id // n_step) & (c_id % n_step <= r_id % n_step)

    def all_steps(q, keys, values):
        s = jnp.where(seen_all, dot_nt(q, keys) * SCALE, NEG_FILL)
        top = jnp.max(s, axis=1, keepdims=True)
        p = jnp.exp2(s - top)
        return dot_nn(p.astype(BF16), values), top, jnp.sum(p, axis=1, keepdims=True)

    q_arr = pack_send[:, :CAPACITY * q_rows].reshape(n_rows, HEAD_DIM)
    o, top, norm = all_steps(q_arr, ks_arr[0], ks_arr[1])
    step_only[...] = (o / norm).astype(BF16).reshape(groups, CAPACITY * q_rows, HEAD_DIM)
    q_res = q_pair[side].reshape(n_rows, HEAD_DIM)
    o, top, norm = all_steps(q_res, ks_res[0], ks_res[1])
    rows3 = (res_rows, q_rows, HEAD_DIM)
    step_part[...] = o.reshape(rows3)
    step_stat[0] = jnp.broadcast_to(top, o.shape).reshape(rows3)
    step_stat[1] = jnp.broadcast_to(norm, o.shape).reshape(rows3)

    for i in range(5, 8):
        prefill(i)
    out_second = out_rows(5, 8, 1)

    part_pair.wait()
    stat_pair.wait()

    def put_row(dst_row, x):
        for a in range(Q_PER_KV):
            dout[dst_row, :, a * HEAD_DIM:(a + 1) * HEAD_DIM] = x[a * n_step:(a + 1) * n_step].astype(BF16)

    def merge(r, carry):
        top_own, top_step = own_stat[0, side, r], step_stat[0, r]
        top_got = jnp.sum(jnp.where(lane == r, stat_recv[0], 0.0), axis=1, keepdims=True)
        norm_got = jnp.sum(jnp.where(lane == r, stat_recv[1], 0.0), axis=1, keepdims=True)
        joint = jnp.maximum(jnp.maximum(top_own, top_step), top_got)
        w_own = jnp.exp2(top_own - joint)
        w_step = jnp.exp2(top_step - joint)
        w_got = jnp.exp2(top_got - joint)
        norm = own_stat[1, side, r] * w_own + step_stat[1, r] * w_step + norm_got * w_got
        x = own_part[side, r] * w_own + step_part[r] * w_step + part_recv[r].astype(F32) * w_got
        put_row(r, x / norm)
        return carry

    lax.fori_loop(0, res_rows, merge, 0, unroll=4)

    def wait_answer(d, carry):
        peer = (me + d) % groups
        pltpu.make_async_remote_copy(
            src_ref=ans_send.at[peer],
            dst_ref=ans_recv.at[peer],
            send_sem=ans_send_sem.at[peer],
            recv_sem=ans_recv_sem.at[peer],
            device_id={"group": peer},
            device_id_type=MESH,
        ).wait()
        return carry

    lax.fori_loop(1, groups, wait_answer, 0)

    def arrive(src, carry):
        count = jnp.int32(0)
        for f in range(finished):
            count = count + jnp.where(owners[src * finished + f] == me, 1, 0)
        for c in range(CAPACITY):
            rows = slice(c * q_rows, (c + 1) * q_rows)
            x = jnp.where(
                count > c, ans_recv[src, rows].astype(F32), step_only[src, rows].astype(F32)
            )
            put_row(res_rows + src * CAPACITY + c, x)
        return carry

    lax.fori_loop(0, groups, arrive, 0, unroll=2)
    out_dec = pltpu.make_async_copy(dout, dout_hbm, out_sem.at[2])
    out_dec.start()
    out_first.wait()
    out_second.wait()
    out_dec.wait()


def per_device(*args):
    q_prefill, kv_fresh, kv_pool, table, lengths, owners, q_decode, kv_steps, kv_res, res_len = args
    groups = lax.axis_size("group")
    rows, n_step, width = q_decode.shape
    res_rows = kv_res.shape[1]
    arr_rows = rows - res_rows
    q_rows = Q_PER_KV * n_step
    seg = q_prefill.shape[0]
    finished = owners.shape[0] // groups
    vmem = pltpu.VMEM
    scratch = [
        vmem(q_prefill.shape, BF16),
        vmem(kv_fresh.shape, BF16),
        vmem(kv_pool.shape, BF16),
        vmem(q_decode.shape, BF16),
        vmem(kv_steps.shape, BF16),
        vmem(kv_res.shape, BF16),
        vmem(q_prefill.shape, BF16),
        vmem(q_decode.shape, BF16),
        vmem((MAXLEN + seg, HEAD_DIM), BF16),
        vmem((MAXLEN + seg, 2 * HEAD_DIM), BF16),
        vmem((STACK * TILE, TILE), F32),
        vmem((2, res_rows, q_rows, HEAD_DIM), BF16),
        vmem((groups, PACK, HEAD_DIM), BF16),
        vmem((groups, PACK, HEAD_DIM), BF16),
        vmem((2, res_rows * n_step, HEAD_DIM), BF16),
        vmem((2, arr_rows * n_step, HEAD_DIM), BF16),
        vmem((res_rows, q_rows, HEAD_DIM), F32),
        vmem((2, res_rows, q_rows, HEAD_DIM), F32),
        vmem((groups, CAPACITY * q_rows, HEAD_DIM), BF16),
        vmem((finished, q_rows, HEAD_DIM), BF16),
        vmem((groups, CAPACITY * q_rows, HEAD_DIM), BF16),
        vmem((groups, CAPACITY * q_rows, HEAD_DIM), BF16),
        vmem((2, res_rows, q_rows, HEAD_DIM), BF16),
        vmem((res_rows, q_rows, HEAD_DIM), BF16),
        vmem((2, q_rows, HEAD_DIM), F32),
        vmem((2, q_rows, HEAD_DIM), F32),
        vmem((2, res_rows, q_rows, HEAD_DIM), F32),
        vmem((2, 2, res_rows, q_rows, HEAD_DIM), F32),
        pltpu.SemaphoreType.DMA((6,)),
        pltpu.SemaphoreType.DMA((3,)),
        pltpu.SemaphoreType.DMA((groups,)),
        pltpu.SemaphoreType.DMA((groups,)),
        pltpu.SemaphoreType.DMA((groups,)),
        pltpu.SemaphoreType.DMA((groups,)),
        pltpu.SemaphoreType.DMA((3,)),
        pltpu.SemaphoreType.DMA((3,)),
    ]
    hbm = pl.BlockSpec(memory_space=pl.ANY)
    smem = pl.BlockSpec(memory_space=pltpu.SMEM)
    return pl.pallas_call(
        functools.partial(kernel, groups),
        out_shape=(
            jax.ShapeDtypeStruct(q_prefill.shape, BF16),
            jax.ShapeDtypeStruct(q_decode.shape, BF16),
        ),
        in_specs=[hbm, hbm, hbm, smem, smem, smem, hbm, hbm, hbm, smem],
        out_specs=(hbm, hbm),
        scratch_shapes=scratch,
        compiler_params=pltpu.CompilerParams(
            collective_id=0, has_side_effects=True, vmem_limit_bytes=56 * 2**20
        ),
        cost_estimate=pl.CostEstimate(
            flops=8 * 10**9, bytes_accessed=21 * 10**6, transcendentals=14 * 10**6
        ),
    )(*args)


def solution(mesh):
    in_specs = (
        P("group", "tp"),
        P(None, "group", "tp"),
        P(None, "group", None, "tp"),
        P("group", None),
        P(),
        P(),
        P("group", None, "tp"),
        P(None, "group", None, "tp"),
        P(None, "group", "tp", None),
        P("group"),
    )
    out_specs = (P("group", "tp"), P("group", None, "tp"))
    return jax.shard_map(
        per_device, mesh=mesh, in_specs=in_specs, out_specs=out_specs, check_vma=False
    )
```

```python
import functools

import jax
import jax.numpy as jnp
from jax import lax
from jax.experimental import pallas as pl
from jax.experimental.pallas import tpu as pltpu
from jax.sharding import PartitionSpec as P

HEAD_DIM = 128
Q_PER_KV = 8
MAXLEN = 1024
CAPACITY = 2
NEG_FILL = -1e30
SCALE = HEAD_DIM ** -0.5 * 1.4426950408889634
PACK = 96
TILE = 128
STACK = 8
BATCH = 8
FIN_BATCH = 4
EARLY = 2
MIDDLE = 5
LAST = 7
MESH = pl.DeviceIdType.MESH
BF16 = jnp.bfloat16
F32 = jnp.float32


def dot_nt(a, b):
    return lax.dot_general(a, b, (((1,), (1,)), ((), ())), preferred_element_type=F32)


def dot_nn(a, b):
    return jnp.dot(a, b, preferred_element_type=F32)


def heads_to_rows(x):
    wide = x.astype(F32)
    parts = [wide[:, a * HEAD_DIM:(a + 1) * HEAD_DIM] for a in range(Q_PER_KV)]
    return jnp.concatenate(parts, axis=0).astype(BF16)


def prefill_block(q_cols, kbuf, vbuf, diag, span):
    q = jnp.concatenate(
        [q_cols[:, h * HEAD_DIM:(h + 1) * HEAD_DIM] for h in range(STACK)], axis=0
    )
    s = dot_nt(q, kbuf[:span])
    s = jnp.concatenate([s[:, :span - TILE], s[:, span - TILE:] + diag[...]], axis=1)
    top = jnp.max(s, axis=1, keepdims=True)
    p = jnp.exp2(s * SCALE - top * SCALE).astype(BF16)
    o = dot_nn(p, vbuf[:span])
    return (o[:, :HEAD_DIM] / o[:, HEAD_DIM:]).astype(BF16)


def fill_diag(diag):
    row = lax.broadcasted_iota(jnp.int32, (STACK * TILE, TILE), 0) % TILE
    col = lax.broadcasted_iota(jnp.int32, (STACK * TILE, TILE), 1)
    diag[...] = jnp.where(col <= row, 0.0, NEG_FILL)


def tail_kernel(qp_hbm, k_hbm, v_hbm, part_hbm, dec_hbm, pout_hbm, dout_hbm, qp, kbuf, vbuf, out, diag, sem):
    done = part_hbm.shape[0]
    rest = pl.ds(done, pout_hbm.shape[0] - done)
    load_q = pltpu.make_async_copy(qp_hbm.at[rest], qp, sem.at[0])
    load_k = pltpu.make_async_copy(k_hbm, kbuf, sem.at[1])
    load_v = pltpu.make_async_copy(v_hbm, vbuf, sem.at[2])
    move_dec = pltpu.make_async_copy(dec_hbm, dout_hbm, sem.at[3])
    move_part = pltpu.make_async_copy(part_hbm, pout_hbm.at[pl.ds(0, done)], sem.at[4])
    for copy in (load_q, load_k, load_v, move_dec, move_part):
        copy.start()
    fill_diag(diag)
    load_q.wait()
    load_k.wait()
    load_v.wait()
    outs = prefill_block(qp[...], kbuf, vbuf, diag, kbuf.shape[0])
    for h in range(STACK):
        out[:, h * HEAD_DIM:(h + 1) * HEAD_DIM] = outs[h * TILE:(h + 1) * TILE]
    store = pltpu.make_async_copy(out, pout_hbm.at[rest], sem.at[5])
    store.start()
    move_dec.wait()
    move_part.wait()
    store.wait()


def kernel(
    groups,
    qp_hbm,
    fresh_hbm,
    pool_hbm,
    table,
    lengths,
    owners,
    qd_hbm,
    steps_hbm,
    res_hbm,
    res_len,
    pout_hbm,
    dout_hbm,
    k_hbm,
    v_hbm,
    qp,
    fresh,
    pool,
    qd,
    steps,
    res,
    pout,
    dout,
    kbuf,
    vbuf,
    diag,
    q_pair,
    pack_send,
    pack_recv,
    ks_res,
    ks_arr,
    step_part,
    step_stat,
    step_only,
    ans,
    ans_send,
    ans_recv,
    part_send,
    part_recv,
    stat_send,
    stat_recv,
    own_part,
    own_stat,
    load_sem,
    out_sem,
    pack_send_sem,
    pack_recv_sem,
    ans_send_sem,
    ans_recv_sem,
    pair_send_sem,
    pair_recv_sem,
):
    me = lax.axis_index("group")
    tp = lax.axis_index("tp")
    side = tp % 2
    partner = tp + 1 - 2 * side
    finished = owners.shape[0] // groups
    res_rows = res.shape[1]
    span_res = res.shape[2]
    n_step = qd.shape[1]
    q_rows = Q_PER_KV * n_step
    seg = qp.shape[0]

    barrier = pltpu.get_barrier_semaphore()

    def greet(d, carry):
        pl.semaphore_signal(
            barrier, inc=1, device_id={"group": (me + d) % groups}, device_id_type=MESH
        )
        return carry

    lax.fori_loop(1, groups, greet, 0)
    pl.semaphore_signal(barrier, inc=1, device_id={"tp": partner}, device_id_type=MESH)

    loads = [
        pltpu.make_async_copy(qd_hbm, qd, load_sem.at[0]),
        pltpu.make_async_copy(steps_hbm, steps, load_sem.at[1]),
        pltpu.make_async_copy(fresh_hbm, fresh, load_sem.at[2]),
        pltpu.make_async_copy(pool_hbm, pool, load_sem.at[3]),
        pltpu.make_async_copy(qp_hbm, qp, load_sem.at[4]),
        pltpu.make_async_copy(res_hbm, res, load_sem.at[5]),
    ]
    for one in loads[:5]:
        one.start()

    loads[0].wait()
    loads[1].wait()

    def relay_res(r, carry):
        q_pair[side, r] = heads_to_rows(qd[r])
        return carry

    lax.fori_loop(0, res_rows, relay_res, 0, unroll=4)

    def relay_arr(o, carry):
        first = res_rows + o * CAPACITY
        for c in range(CAPACITY):
            pack_send[o, c * q_rows:(c + 1) * q_rows] = heads_to_rows(qd[first + c])
        for k in range(2):
            rows = [steps[k, first + c].astype(F32) for c in range(CAPACITY)]
            rows.append(jnp.zeros((16 - CAPACITY * n_step, HEAD_DIM), F32))
            start = CAPACITY * q_rows + 16 * k
            pack_send[o, start:start + 16] = jnp.concatenate(rows, axis=0).astype(BF16)
        return carry

    lax.fori_loop(0, groups, relay_arr, 0, unroll=2)

    per_tile = 16 // n_step

    def gather_steps(i, carry):
        for k in range(2):
            for base, dst in ((0, ks_res), (res_rows, ks_arr)):
                rows = [steps[k, base + i * per_tile + c].astype(F32) for c in range(per_tile)]
                dst[k, pl.ds(pl.multiple_of(i * 16, 16), 16)] = jnp.concatenate(
                    rows, axis=0
                ).astype(BF16)
        return carry

    lax.fori_loop(0, res_rows // per_tile, gather_steps, 0, unroll=2)

    loads[2].wait()
    loads[3].wait()
    loads[5].start()
    ctx_len = lengths[me * (finished + 1) + finished]
    first_key = pool[0, table[finished, 0]][0:1]
    block = pool.shape[2]
    for b in range(MAXLEN // block):
        blk = table[finished, b]
        valid = lax.broadcasted_iota(jnp.int32, (block, HEAD_DIM), 0) + b * block < ctx_len
        kbuf[b * block:(b + 1) * block] = jnp.where(
            valid, pool[0, blk].astype(F32), first_key.astype(F32)
        ).astype(BF16)
        vbuf[b * block:(b + 1) * block, :HEAD_DIM] = jnp.where(
            valid, pool[1, blk].astype(F32), 0.0
        ).astype(BF16)
        vbuf[b * block:(b + 1) * block, HEAD_DIM:] = jnp.where(valid, 1.0, 0.0).astype(BF16)
    kbuf[MAXLEN:] = fresh[0]
    vbuf[MAXLEN:, :HEAD_DIM] = fresh[1]
    vbuf[MAXLEN:, HEAD_DIM:] = jnp.ones((seg, HEAD_DIM), BF16)
    fill_diag(diag)
    keys_out = pltpu.make_async_copy(kbuf, k_hbm, out_sem.at[3])
    keys_out.start()
    values_out = pltpu.make_async_copy(vbuf, v_hbm, out_sem.at[4])
    values_out.start()
    loads[4].wait()

    def prefill(i):
        rows = slice(i * TILE, (i + 1) * TILE)
        outs = prefill_block(qp[rows], kbuf, vbuf, diag, MAXLEN + (i + 1) * TILE)
        for h in range(STACK):
            pout[rows, h * HEAD_DIM:(h + 1) * HEAD_DIM] = outs[h * TILE:(h + 1) * TILE]

    def out_rows(first, last, i):
        rows = pl.ds(first * TILE, (last - first) * TILE)
        copy = pltpu.make_async_copy(pout.at[rows], pout_hbm.at[rows], out_sem.at[i])
        copy.start()
        return copy

    for i in range(EARLY):
        prefill(i)

    pl.semaphore_wait(barrier, groups)

    def pack_copy(peer):
        return pltpu.make_async_remote_copy(
            src_ref=pack_send.at[peer],
            dst_ref=pack_recv.at[me],
            send_sem=pack_send_sem.at[peer],
            recv_sem=pack_recv_sem.at[me],
            device_id={"group": peer},
            device_id_type=MESH,
        )

    def pair_copy(src, dst, i):
        return pltpu.make_async_remote_copy(
            src_ref=src,
            dst_ref=dst,
            send_sem=pair_send_sem.at[i],
            recv_sem=pair_recv_sem.at[i],
            device_id={"tp": partner},
            device_id_type=MESH,
        )

    q_copy = pair_copy(q_pair.at[side], q_pair.at[side], 0)
    q_copy.start()

    def send_pack(d, carry):
        pack_copy((me + d) % groups).start()
        return carry

    lax.fori_loop(1, groups, send_pack, 0)
    pack_recv[me] = pack_send[me]


    for i in range(EARLY, MIDDLE):
        prefill(i)
    out_first = out_rows(0, MIDDLE, 0)

    loads[5].wait()
    q_copy.wait()
    lane = lax.broadcasted_iota(jnp.int32, (q_rows, HEAD_DIM), 1)
    position = side * span_res + lax.broadcasted_iota(jnp.int32, (2 * q_rows, span_res), 1)
    empty = jnp.zeros((q_rows, HEAD_DIM), BF16)

    def resident_rows(i, carry):
        tops, norms = carry
        rows = [i * BATCH + b for b in range(BATCH)]
        scores = []
        for r in rows:
            q = jnp.concatenate(
                [
                    jnp.concatenate([q_pair[0, r], empty], axis=1),
                    jnp.concatenate([empty, q_pair[1, r]], axis=1),
                ],
                axis=0,
            )
            scores.append(dot_nt(q, res[0, r]))
        scores = [
            jnp.where(position < res_len[r], s * SCALE, NEG_FILL) for r, s in zip(rows, scores)
        ]
        maxima = [jnp.max(s, axis=1, keepdims=True) for s in scores]
        weights = [jnp.exp2(s - m) for s, m in zip(scores, maxima)]
        sums = [jnp.sum(p, axis=1, keepdims=True) for p in weights]
        outs = [dot_nn(p.astype(BF16), res[1, r]) for r, p in zip(rows, weights)]
        for r, m, l, o in zip(rows, maxima, sums, outs):
            for u in range(2):
                head = slice(u * q_rows, (u + 1) * q_rows)
                part = o[head, u * HEAD_DIM:(u + 1) * HEAD_DIM]
                own_part[u, r] = part
                part_send[u, r] = part.astype(BF16)
                own_stat[0, u, r] = jnp.broadcast_to(m[head], (q_rows, HEAD_DIM))
                own_stat[1, u, r] = jnp.broadcast_to(l[head], (q_rows, HEAD_DIM))
            give = jnp.where(side == 0, m[q_rows:], m[:q_rows])
            tops = jnp.where(lane == r, give, tops)
            give = jnp.where(side == 0, l[q_rows:], l[:q_rows])
            norms = jnp.where(lane == r, give, norms)
        return tops, norms

    zeros = jnp.zeros((q_rows, HEAD_DIM), F32)
    tops, norms = lax.fori_loop(0, res_rows // BATCH, resident_rows, (zeros, zeros))
    stat_send[0] = tops
    stat_send[1] = norms
    part_pair = pair_copy(part_send.at[1 - side], part_recv, 1)
    part_pair.start()
    stat_pair = pair_copy(stat_send, stat_recv, 2)
    stat_pair.start()

    def wait_pack(d, carry):
        peer = (me + d) % groups
        pltpu.make_async_remote_copy(
            src_ref=pack_send.at[peer],
            dst_ref=pack_recv.at[peer],
            send_sem=pack_send_sem.at[peer],
            recv_sem=pack_recv_sem.at[peer],
            device_id={"group": peer},
            device_id_type=MESH,
        ).wait()
        return carry

    lax.fori_loop(1, groups, wait_pack, 0)

    owner_of = [owners[me * finished + f] for f in range(finished)]
    slot_of = []
    for f in range(finished):
        rank = jnp.int32(0)
        for f2 in range(f):
            rank = rank + jnp.where(owner_of[f2] == owner_of[f], 1, 0)
        slot_of.append(owner_of[f] * CAPACITY + rank)

    cache_pos = lax.broadcasted_iota(jnp.int32, (q_rows, MAXLEN), 1)
    step_row = lax.broadcasted_iota(jnp.int32, (q_rows, 16), 0) % n_step
    step_col = lax.broadcasted_iota(jnp.int32, (q_rows, 16), 1)

    def finished_rows(batch):
        scores, step_scores, step_values = [], [], []
        for f in batch:
            owner = owner_of[f]
            rank = slot_of[f] - owner * CAPACITY
            q = jnp.where(
                rank == 0,
                pack_recv[owner, 0:q_rows].astype(F32),
                pack_recv[owner, q_rows:2 * q_rows].astype(F32),
            ).astype(BF16)
            keys = jnp.concatenate([pool[0, table[f, b]] for b in range(MAXLEN // block)], axis=0)
            length = lengths[me * (finished + 1) + f]
            scores.append(jnp.where(cache_pos < length, dot_nt(q, keys) * SCALE, NEG_FILL))
            seen = (step_col // n_step == rank) & (step_col % n_step <= step_row)
            step_k = pack_recv[owner, 2 * q_rows:2 * q_rows + 16]
            step_scores.append(jnp.where(seen, dot_nt(q, step_k) * SCALE, NEG_FILL))
            step_values.append(pack_recv[owner, 2 * q_rows + 16:2 * q_rows + 32])
        maxima = [
            jnp.maximum(jnp.max(s, axis=1, keepdims=True), jnp.max(s2, axis=1, keepdims=True))
            for s, s2 in zip(scores, step_scores)
        ]
        weights = [jnp.exp2(s - m) for s, m in zip(scores, maxima)]
        step_weights = [jnp.exp2(s - m) for s, m in zip(step_scores, maxima)]
        sums = [
            jnp.sum(p, axis=1, keepdims=True) + jnp.sum(p2, axis=1, keepdims=True)
            for p, p2 in zip(weights, step_weights)
        ]
        for f, p, p2, v2, l in zip(batch, weights, step_weights, step_values, sums):
            values = jnp.concatenate([pool[1, table[f, b]] for b in range(MAXLEN // block)], axis=0)
            o = dot_nn(p.astype(BF16), values) + dot_nn(p2.astype(BF16), v2)
            ans[f] = (o / l).astype(BF16)

    for first in range(0, finished, FIN_BATCH):
        finished_rows(range(first, min(first + FIN_BATCH, finished)))

    for n in range(groups * CAPACITY):
        f = jnp.int32(0)
        for j in range(1, finished):
            f = f + jnp.where(slot_of[j] == n, j, 0)
        ans_send[n // CAPACITY, (n % CAPACITY) * q_rows:(n % CAPACITY + 1) * q_rows] = ans[f]

    def send_answer(d, carry):
        peer = (me + d) % groups
        pltpu.make_async_remote_copy(
            src_ref=ans_send.at[peer],
            dst_ref=ans_recv.at[me],
            send_sem=ans_send_sem.at[peer],
            recv_sem=ans_recv_sem.at[me],
            device_id={"group": peer},
            device_id_type=MESH,
        ).start()
        return carry

    lax.fori_loop(1, groups, send_answer, 0)
    ans_recv[me] = ans_send[me]


    n_rows, n_cols = res_rows * q_rows, res_rows * n_step
    r_id = lax.broadcasted_iota(jnp.int32, (n_rows, n_cols), 0)
    c_id = lax.broadcasted_iota(jnp.int32, (n_rows, n_cols), 1)
    seen_all = (r_id // q_rows == c_id // n_step) & (c_id % n_step <= r_id % n_step)

    def all_steps(q, keys, values):
        s = jnp.where(seen_all, dot_nt(q, keys) * SCALE, NEG_FILL)
        top = jnp.max(s, axis=1, keepdims=True)
        p = jnp.exp2(s - top)
        return dot_nn(p.astype(BF16), values), top, jnp.sum(p, axis=1, keepdims=True)

    q_arr = pack_send[:, :CAPACITY * q_rows].reshape(n_rows, HEAD_DIM)
    o, top, norm = all_steps(q_arr, ks_arr[0], ks_arr[1])
    step_only[...] = (o / norm).astype(BF16).reshape(groups, CAPACITY * q_rows, HEAD_DIM)
    q_res = q_pair[side].reshape(n_rows, HEAD_DIM)
    o, top, norm = all_steps(q_res, ks_res[0], ks_res[1])
    rows3 = (res_rows, q_rows, HEAD_DIM)
    step_part[...] = o.reshape(rows3)
    step_stat[0] = jnp.broadcast_to(top, o.shape).reshape(rows3)
    step_stat[1] = jnp.broadcast_to(norm, o.shape).reshape(rows3)

    for i in range(MIDDLE, LAST):
        prefill(i)
    out_second = out_rows(MIDDLE, LAST, 1)

    part_pair.wait()
    stat_pair.wait()

    def put_row(dst_row, x):
        for a in range(Q_PER_KV):
            dout[dst_row, :, a * HEAD_DIM:(a + 1) * HEAD_DIM] = x[a * n_step:(a + 1) * n_step].astype(BF16)

    def merge(r, carry):
        top_own, top_step = own_stat[0, side, r], step_stat[0, r]
        top_got = jnp.sum(jnp.where(lane == r, stat_recv[0], 0.0), axis=1, keepdims=True)
        norm_got = jnp.sum(jnp.where(lane == r, stat_recv[1], 0.0), axis=1, keepdims=True)
        joint = jnp.maximum(jnp.maximum(top_own, top_step), top_got)
        w_own = jnp.exp2(top_own - joint)
        w_step = jnp.exp2(top_step - joint)
        w_got = jnp.exp2(top_got - joint)
        norm = own_stat[1, side, r] * w_own + step_stat[1, r] * w_step + norm_got * w_got
        x = own_part[side, r] * w_own + step_part[r] * w_step + part_recv[r].astype(F32) * w_got
        put_row(r, x / norm)
        return carry

    lax.fori_loop(0, res_rows, merge, 0, unroll=4)

    def wait_answer(d, carry):
        peer = (me + d) % groups
        pltpu.make_async_remote_copy(
            src_ref=ans_send.at[peer],
            dst_ref=ans_recv.at[peer],
            send_sem=ans_send_sem.at[peer],
            recv_sem=ans_recv_sem.at[peer],
            device_id={"group": peer},
            device_id_type=MESH,
        ).wait()
        return carry

    lax.fori_loop(1, groups, wait_answer, 0)

    def arrive(src, carry):
        count = jnp.int32(0)
        for f in range(finished):
            count = count + jnp.where(owners[src * finished + f] == me, 1, 0)
        for c in range(CAPACITY):
            rows = slice(c * q_rows, (c + 1) * q_rows)
            x = jnp.where(
                count > c, ans_recv[src, rows].astype(F32), step_only[src, rows].astype(F32)
            )
            put_row(res_rows + src * CAPACITY + c, x)
        return carry

    lax.fori_loop(0, groups, arrive, 0, unroll=2)
    out_dec = pltpu.make_async_copy(dout, dout_hbm, out_sem.at[2])
    out_dec.start()
    out_first.wait()
    out_second.wait()
    out_dec.wait()
    keys_out.wait()
    values_out.wait()


def per_device(*args):
    q_prefill, kv_fresh, kv_pool, table, lengths, owners, q_decode, kv_steps, kv_res, res_len = args
    groups = lax.axis_size("group")
    rows, n_step, width = q_decode.shape
    res_rows = kv_res.shape[1]
    arr_rows = rows - res_rows
    q_rows = Q_PER_KV * n_step
    seg = q_prefill.shape[0]
    finished = owners.shape[0] // groups
    vmem = pltpu.VMEM
    scratch = [
        vmem(q_prefill.shape, BF16),
        vmem(kv_fresh.shape, BF16),
        vmem(kv_pool.shape, BF16),
        vmem(q_decode.shape, BF16),
        vmem(kv_steps.shape, BF16),
        vmem(kv_res.shape, BF16),
        vmem((LAST * TILE, q_prefill.shape[1]), BF16),
        vmem(q_decode.shape, BF16),
        vmem((MAXLEN + seg, HEAD_DIM), BF16),
        vmem((MAXLEN + seg, 2 * HEAD_DIM), BF16),
        vmem((STACK * TILE, TILE), F32),
        vmem((2, res_rows, q_rows, HEAD_DIM), BF16),
        vmem((groups, PACK, HEAD_DIM), BF16),
        vmem((groups, PACK, HEAD_DIM), BF16),
        vmem((2, res_rows * n_step, HEAD_DIM), BF16),
        vmem((2, arr_rows * n_step, HEAD_DIM), BF16),
        vmem((res_rows, q_rows, HEAD_DIM), F32),
        vmem((2, res_rows, q_rows, HEAD_DIM), F32),
        vmem((groups, CAPACITY * q_rows, HEAD_DIM), BF16),
        vmem((finished, q_rows, HEAD_DIM), BF16),
        vmem((groups, CAPACITY * q_rows, HEAD_DIM), BF16),
        vmem((groups, CAPACITY * q_rows, HEAD_DIM), BF16),
        vmem((2, res_rows, q_rows, HEAD_DIM), BF16),
        vmem((res_rows, q_rows, HEAD_DIM), BF16),
        vmem((2, q_rows, HEAD_DIM), F32),
        vmem((2, q_rows, HEAD_DIM), F32),
        vmem((2, res_rows, q_rows, HEAD_DIM), F32),
        vmem((2, 2, res_rows, q_rows, HEAD_DIM), F32),
        pltpu.SemaphoreType.DMA((6,)),
        pltpu.SemaphoreType.DMA((5,)),
        pltpu.SemaphoreType.DMA((groups,)),
        pltpu.SemaphoreType.DMA((groups,)),
        pltpu.SemaphoreType.DMA((groups,)),
        pltpu.SemaphoreType.DMA((groups,)),
        pltpu.SemaphoreType.DMA((3,)),
        pltpu.SemaphoreType.DMA((3,)),
    ]
    hbm = pl.BlockSpec(memory_space=pl.ANY)
    smem = pl.BlockSpec(memory_space=pltpu.SMEM)
    keys = jax.ShapeDtypeStruct((MAXLEN + seg, HEAD_DIM), BF16)
    values = jax.ShapeDtypeStruct((MAXLEN + seg, 2 * HEAD_DIM), BF16)
    pre_out = jax.ShapeDtypeStruct(q_prefill.shape, BF16)
    dec_out = jax.ShapeDtypeStruct(q_decode.shape, BF16)
    part, dec, k_all, v_all = pl.pallas_call(
        functools.partial(kernel, groups),
        out_shape=(
            jax.ShapeDtypeStruct((LAST * TILE, q_prefill.shape[1]), BF16),
            dec_out,
            keys,
            values,
        ),
        in_specs=[hbm, hbm, hbm, smem, smem, smem, hbm, hbm, hbm, smem],
        out_specs=(hbm,) * 4,
        scratch_shapes=scratch,
        compiler_params=pltpu.CompilerParams(
            collective_id=0, has_side_effects=True, vmem_limit_bytes=56 * 2**20
        ),
        cost_estimate=pl.CostEstimate(
            flops=8 * 10**9, bytes_accessed=21 * 10**6, transcendentals=14 * 10**6
        ),
    )(*args)
    last = seg - LAST * TILE
    return pl.pallas_call(
        tail_kernel,
        out_shape=(pre_out, dec_out),
        in_specs=[hbm] * 5,
        out_specs=(hbm, hbm),
        scratch_shapes=[
            vmem((last, q_prefill.shape[1]), BF16),
            vmem(keys.shape, BF16),
            vmem(values.shape, BF16),
            vmem((last, q_prefill.shape[1]), BF16),
            vmem((STACK * TILE, TILE), F32),
            pltpu.SemaphoreType.DMA((6,)),
        ],
        compiler_params=pltpu.CompilerParams(vmem_limit_bytes=56 * 2**20),
        cost_estimate=pl.CostEstimate(
            flops=10**9, bytes_accessed=8 * 10**6, transcendentals=2 * 10**6
        ),
    )(q_prefill, k_all, v_all, part, dec)


def solution(mesh):
    in_specs = (
        P("group", "tp"),
        P(None, "group", "tp"),
        P(None, "group", None, "tp"),
        P("group", None),
        P(),
        P(),
        P("group", None, "tp"),
        P(None, "group", None, "tp"),
        P(None, "group", "tp", None),
        P("group"),
    )
    out_specs = (P("group", "tp"), P("group", None, "tp"))
    return jax.shard_map(
        per_device, mesh=mesh, in_specs=in_specs, out_specs=out_specs, check_vma=False
    )
```

```python
import functools

import jax
import jax.numpy as jnp
from jax import lax
from jax.experimental import pallas as pl
from jax.experimental.pallas import tpu as pltpu
from jax.sharding import PartitionSpec as P

HEAD_DIM = 128
Q_PER_KV = 8
MAXLEN = 1024
CAPACITY = 2
NEG_FILL = -1e30
SCALE = HEAD_DIM ** -0.5 * 1.4426950408889634
PACK = 96
TILE = 128
STACK = 8
BATCH = 8
FIN_BATCH = 4
EARLY = 1
MIDDLE = 5
AHEAD = 0
MESH = pl.DeviceIdType.MESH
BF16 = jnp.bfloat16
F32 = jnp.float32


def dot_nt(a, b):
    return lax.dot_general(a, b, (((1,), (1,)), ((), ())), preferred_element_type=F32)


def dot_nn(a, b):
    return jnp.dot(a, b, preferred_element_type=F32)


def heads_to_rows(x):
    wide = x.astype(F32)
    parts = [wide[:, a * HEAD_DIM:(a + 1) * HEAD_DIM] for a in range(Q_PER_KV)]
    return jnp.concatenate(parts, axis=0).astype(BF16)


def stacked(q_cols):
    return jnp.concatenate(
        [q_cols[:, h * HEAD_DIM:(h + 1) * HEAD_DIM] for h in range(STACK)], axis=0
    )


def causal_scores(q, keys, diag):
    s = dot_nt(q, keys)
    edge = s.shape[1] - TILE
    if edge == 0:
        return s + diag[...]
    return jnp.concatenate([s[:, :edge], s[:, edge:] + diag[...]], axis=1)


def weigh(s, top, values):
    return dot_nn(jnp.exp2((s - top) * SCALE).astype(BF16), values)


def row_max(s):
    return jnp.max(s, axis=1, keepdims=True)


def normalized(o):
    return (o[:, :HEAD_DIM] / o[:, HEAD_DIM:]).astype(BF16)


def fill_diag(diag):
    row = lax.broadcasted_iota(jnp.int32, (STACK * TILE, TILE), 0) % TILE
    col = lax.broadcasted_iota(jnp.int32, (STACK * TILE, TILE), 1)
    diag[...] = jnp.where(col <= row, 0.0, NEG_FILL)


def kernel(
    groups,
    qp_hbm,
    fresh_hbm,
    pool_hbm,
    table,
    lengths,
    owners,
    qd_hbm,
    steps_hbm,
    res_hbm,
    res_len,
    pout_hbm,
    dout_hbm,
    qp,
    fresh,
    pool,
    qd,
    steps,
    res,
    pout,
    dout,
    kbuf,
    vbuf,
    diag,
    ahead_sum,
    ahead_top,
    q_pair,
    pack_send,
    pack_recv,
    ks_res,
    ks_arr,
    step_part,
    step_stat,
    step_only,
    ans,
    ans_send,
    ans_recv,
    part_send,
    part_recv,
    stat_send,
    stat_recv,
    own_part,
    own_stat,
    load_sem,
    out_sem,
    pack_send_sem,
    pack_recv_sem,
    ans_send_sem,
    ans_recv_sem,
    pair_send_sem,
    pair_recv_sem,
):
    me = lax.axis_index("group")
    tp = lax.axis_index("tp")
    side = tp % 2
    partner = tp + 1 - 2 * side
    finished = owners.shape[0] // groups
    res_rows = res.shape[1]
    span_res = res.shape[2]
    n_step = qd.shape[1]
    q_rows = Q_PER_KV * n_step
    seg = qp.shape[0]

    barrier = pltpu.get_barrier_semaphore()

    def greet(d, carry):
        pl.semaphore_signal(
            barrier, inc=1, device_id={"group": (me + d) % groups}, device_id_type=MESH
        )
        return carry

    lax.fori_loop(1, groups, greet, 0)
    pl.semaphore_signal(barrier, inc=1, device_id={"tp": partner}, device_id_type=MESH)

    loads = [
        pltpu.make_async_copy(qd_hbm, qd, load_sem.at[0]),
        pltpu.make_async_copy(steps_hbm, steps, load_sem.at[1]),
        pltpu.make_async_copy(fresh_hbm, fresh, load_sem.at[2]),
        pltpu.make_async_copy(pool_hbm, pool, load_sem.at[3]),
        pltpu.make_async_copy(qp_hbm, qp, load_sem.at[4]),
        pltpu.make_async_copy(res_hbm, res, load_sem.at[5]),
    ]
    for i in (0, 1, 2, 4):
        loads[i].start()

    loads[0].wait()
    loads[1].wait()
    loads[3].start()

    def relay_res(r, carry):
        q_pair[side, r] = heads_to_rows(qd[r])
        return carry

    lax.fori_loop(0, res_rows, relay_res, 0, unroll=4)

    def relay_arr(o, carry):
        first = res_rows + o * CAPACITY
        for c in range(CAPACITY):
            pack_send[o, c * q_rows:(c + 1) * q_rows] = heads_to_rows(qd[first + c])
        for k in range(2):
            rows = [steps[k, first + c].astype(F32) for c in range(CAPACITY)]
            rows.append(jnp.zeros((16 - CAPACITY * n_step, HEAD_DIM), F32))
            start = CAPACITY * q_rows + 16 * k
            pack_send[o, start:start + 16] = jnp.concatenate(rows, axis=0).astype(BF16)
        return carry

    lax.fori_loop(0, groups, relay_arr, 0, unroll=2)

    per_tile = 16 // n_step

    def gather_steps(i, carry):
        for k in range(2):
            for base, dst in ((0, ks_res), (res_rows, ks_arr)):
                rows = [steps[k, base + i * per_tile + c].astype(F32) for c in range(per_tile)]
                dst[k, pl.ds(pl.multiple_of(i * 16, 16), 16)] = jnp.concatenate(
                    rows, axis=0
                ).astype(BF16)
        return carry

    lax.fori_loop(0, res_rows // per_tile, gather_steps, 0, unroll=2)

    loads[2].wait()
    kbuf[MAXLEN:] = fresh[0]
    vbuf[MAXLEN:, :HEAD_DIM] = fresh[1]
    vbuf[MAXLEN:, HEAD_DIM:] = jnp.ones((seg, HEAD_DIM), BF16)
    fill_diag(diag)
    loads[4].wait()

    for i in range(AHEAD):
        span = (i + 1) * TILE
        s = causal_scores(stacked(qp[i * TILE:span]), kbuf[MAXLEN:MAXLEN + span], diag)
        top = row_max(s)
        ahead_top[i] = jnp.broadcast_to(top, (STACK * TILE, HEAD_DIM))
        ahead_sum[i] = weigh(s, top, vbuf[MAXLEN:MAXLEN + span])

    loads[3].wait()
    loads[5].start()
    ctx_len = lengths[me * (finished + 1) + finished]
    first_key = pool[0, table[finished, 0]][0:1]
    block = pool.shape[2]
    for b in range(MAXLEN // block):
        blk = table[finished, b]
        valid = lax.broadcasted_iota(jnp.int32, (block, HEAD_DIM), 0) + b * block < ctx_len
        kbuf[b * block:(b + 1) * block] = jnp.where(
            valid, pool[0, blk].astype(F32), first_key.astype(F32)
        ).astype(BF16)
        vbuf[b * block:(b + 1) * block, :HEAD_DIM] = jnp.where(
            valid, pool[1, blk].astype(F32), 0.0
        ).astype(BF16)
        vbuf[b * block:(b + 1) * block, HEAD_DIM:] = jnp.where(valid, 1.0, 0.0).astype(BF16)

    def prefill_scores(i):
        q = stacked(qp[i * TILE:(i + 1) * TILE])
        if i < AHEAD:
            return dot_nt(q, kbuf[:MAXLEN])
        return causal_scores(q, kbuf[:MAXLEN + (i + 1) * TILE], diag)

    def prefill_rest(i, s):
        rows = slice(i * TILE, (i + 1) * TILE)
        if i < AHEAD:
            top = jnp.maximum(jnp.broadcast_to(row_max(s), (STACK * TILE, HEAD_DIM)), ahead_top[i])
            w = jnp.exp2((ahead_top[i] - top) * SCALE)
            o = weigh(s, top[:, :1], vbuf[:MAXLEN])
            o = o + ahead_sum[i] * jnp.concatenate([w, w], axis=1)
        else:
            o = weigh(s, row_max(s), vbuf[:MAXLEN + (i + 1) * TILE])
        outs = normalized(o)
        for h in range(STACK):
            pout[rows, h * HEAD_DIM:(h + 1) * HEAD_DIM] = outs[h * TILE:(h + 1) * TILE]

    def prefill(first, last, s=None, after=False):
        if s is None:
            s = prefill_scores(first)
        for i in range(first, last):
            ahead = prefill_scores(i + 1) if after or i + 1 < last else None
            prefill_rest(i, s)
            s = ahead
        return s

    def out_rows(first, last, i):
        rows = pl.ds(first * TILE, (last - first) * TILE)
        copy = pltpu.make_async_copy(pout.at[rows], pout_hbm.at[rows], out_sem.at[i])
        copy.start()
        return copy

    scores = prefill(0, EARLY, after=True)

    pl.semaphore_wait(barrier, groups)

    def pack_copy(peer):
        return pltpu.make_async_remote_copy(
            src_ref=pack_send.at[peer],
            dst_ref=pack_recv.at[me],
            send_sem=pack_send_sem.at[peer],
            recv_sem=pack_recv_sem.at[me],
            device_id={"group": peer},
            device_id_type=MESH,
        )

    def pair_copy(src, dst, i):
        return pltpu.make_async_remote_copy(
            src_ref=src,
            dst_ref=dst,
            send_sem=pair_send_sem.at[i],
            recv_sem=pair_recv_sem.at[i],
            device_id={"tp": partner},
            device_id_type=MESH,
        )

    q_copy = pair_copy(q_pair.at[side], q_pair.at[side], 0)
    q_copy.start()

    def send_pack(d, carry):
        pack_copy((me + d) % groups).start()
        return carry

    lax.fori_loop(1, groups, send_pack, 0)
    pack_recv[me] = pack_send[me]


    prefill(EARLY, MIDDLE, scores)
    out_first = out_rows(0, MIDDLE, 0)

    loads[5].wait()
    q_copy.wait()
    lane = lax.broadcasted_iota(jnp.int32, (q_rows, HEAD_DIM), 1)
    position = side * span_res + lax.broadcasted_iota(jnp.int32, (2 * q_rows, span_res), 1)
    empty = jnp.zeros((q_rows, HEAD_DIM), BF16)

    def resident_rows(i, carry):
        tops, norms = carry
        rows = [i * BATCH + b for b in range(BATCH)]
        scores = []
        for r in rows:
            q = jnp.concatenate(
                [
                    jnp.concatenate([q_pair[0, r], empty], axis=1),
                    jnp.concatenate([empty, q_pair[1, r]], axis=1),
                ],
                axis=0,
            )
            scores.append(dot_nt(q, res[0, r]))
        scores = [
            jnp.where(position < res_len[r], s * SCALE, NEG_FILL) for r, s in zip(rows, scores)
        ]
        maxima = [jnp.max(s, axis=1, keepdims=True) for s in scores]
        weights = [jnp.exp2(s - m) for s, m in zip(scores, maxima)]
        sums = [jnp.sum(p, axis=1, keepdims=True) for p in weights]
        outs = [dot_nn(p.astype(BF16), res[1, r]) for r, p in zip(rows, weights)]
        for r, m, l, o in zip(rows, maxima, sums, outs):
            for u in range(2):
                head = slice(u * q_rows, (u + 1) * q_rows)
                part = o[head, u * HEAD_DIM:(u + 1) * HEAD_DIM]
                own_part[u, r] = part
                part_send[u, r] = part.astype(BF16)
                own_stat[0, u, r] = jnp.broadcast_to(m[head], (q_rows, HEAD_DIM))
                own_stat[1, u, r] = jnp.broadcast_to(l[head], (q_rows, HEAD_DIM))
            give = jnp.where(side == 0, m[q_rows:], m[:q_rows])
            tops = jnp.where(lane == r, give, tops)
            give = jnp.where(side == 0, l[q_rows:], l[:q_rows])
            norms = jnp.where(lane == r, give, norms)
        return tops, norms

    zeros = jnp.zeros((q_rows, HEAD_DIM), F32)
    tops, norms = zeros, zeros
    for i in range(res_rows // BATCH):
        tops, norms = resident_rows(i, (tops, norms))
    stat_send[0] = tops
    stat_send[1] = norms
    part_pair = pair_copy(part_send.at[1 - side], part_recv, 1)
    part_pair.start()
    stat_pair = pair_copy(stat_send, stat_recv, 2)
    stat_pair.start()

    def wait_pack(d, carry):
        peer = (me + d) % groups
        pltpu.make_async_remote_copy(
            src_ref=pack_send.at[peer],
            dst_ref=pack_recv.at[peer],
            send_sem=pack_send_sem.at[peer],
            recv_sem=pack_recv_sem.at[peer],
            device_id={"group": peer},
            device_id_type=MESH,
        ).wait()
        return carry

    lax.fori_loop(1, groups, wait_pack, 0)

    owner_of = [owners[me * finished + f] for f in range(finished)]
    slot_of = []
    for f in range(finished):
        rank = jnp.int32(0)
        for f2 in range(f):
            rank = rank + jnp.where(owner_of[f2] == owner_of[f], 1, 0)
        slot_of.append(owner_of[f] * CAPACITY + rank)

    cache_pos = lax.broadcasted_iota(jnp.int32, (q_rows, MAXLEN), 1)
    step_row = lax.broadcasted_iota(jnp.int32, (q_rows, 16), 0) % n_step
    step_col = lax.broadcasted_iota(jnp.int32, (q_rows, 16), 1)

    def finished_rows(batch):
        scores, step_scores, step_values = [], [], []
        for f in batch:
            owner = owner_of[f]
            rank = slot_of[f] - owner * CAPACITY
            q = jnp.where(
                rank == 0,
                pack_recv[owner, 0:q_rows].astype(F32),
                pack_recv[owner, q_rows:2 * q_rows].astype(F32),
            ).astype(BF16)
            keys = jnp.concatenate([pool[0, table[f, b]] for b in range(MAXLEN // block)], axis=0)
            length = lengths[me * (finished + 1) + f]
            scores.append(jnp.where(cache_pos < length, dot_nt(q, keys) * SCALE, NEG_FILL))
            seen = (step_col // n_step == rank) & (step_col % n_step <= step_row)
            step_k = pack_recv[owner, 2 * q_rows:2 * q_rows + 16]
            step_scores.append(jnp.where(seen, dot_nt(q, step_k) * SCALE, NEG_FILL))
            step_values.append(pack_recv[owner, 2 * q_rows + 16:2 * q_rows + 32])
        maxima = [
            jnp.maximum(jnp.max(s, axis=1, keepdims=True), jnp.max(s2, axis=1, keepdims=True))
            for s, s2 in zip(scores, step_scores)
        ]
        weights = [jnp.exp2(s - m) for s, m in zip(scores, maxima)]
        step_weights = [jnp.exp2(s - m) for s, m in zip(step_scores, maxima)]
        sums = [
            jnp.sum(p, axis=1, keepdims=True) + jnp.sum(p2, axis=1, keepdims=True)
            for p, p2 in zip(weights, step_weights)
        ]
        for f, p, p2, v2, l in zip(batch, weights, step_weights, step_values, sums):
            values = jnp.concatenate([pool[1, table[f, b]] for b in range(MAXLEN // block)], axis=0)
            o = dot_nn(p.astype(BF16), values) + dot_nn(p2.astype(BF16), v2)
            ans[f] = (o / l).astype(BF16)

    next_scores = prefill_scores(MIDDLE)
    for first in range(0, finished, FIN_BATCH):
        finished_rows(range(first, min(first + FIN_BATCH, finished)))

    for n in range(groups * CAPACITY):
        f = jnp.int32(0)
        for j in range(1, finished):
            f = f + jnp.where(slot_of[j] == n, j, 0)
        ans_send[n // CAPACITY, (n % CAPACITY) * q_rows:(n % CAPACITY + 1) * q_rows] = ans[f]

    def send_answer(d, carry):
        peer = (me + d) % groups
        pltpu.make_async_remote_copy(
            src_ref=ans_send.at[peer],
            dst_ref=ans_recv.at[me],
            send_sem=ans_send_sem.at[peer],
            recv_sem=ans_recv_sem.at[me],
            device_id={"group": peer},
            device_id_type=MESH,
        ).start()
        return carry

    lax.fori_loop(1, groups, send_answer, 0)
    ans_recv[me] = ans_send[me]


    n_rows, n_cols = res_rows * q_rows, res_rows * n_step
    r_id = lax.broadcasted_iota(jnp.int32, (n_rows, n_cols), 0)
    c_id = lax.broadcasted_iota(jnp.int32, (n_rows, n_cols), 1)
    seen_all = (r_id // q_rows == c_id // n_step) & (c_id % n_step <= r_id % n_step)

    def all_steps(q, keys, values):
        s = jnp.where(seen_all, dot_nt(q, keys) * SCALE, NEG_FILL)
        top = jnp.max(s, axis=1, keepdims=True)
        p = jnp.exp2(s - top)
        return dot_nn(p.astype(BF16), values), top, jnp.sum(p, axis=1, keepdims=True)

    q_arr = pack_send[:, :CAPACITY * q_rows].reshape(n_rows, HEAD_DIM)
    o, top, norm = all_steps(q_arr, ks_arr[0], ks_arr[1])
    step_only[...] = (o / norm).astype(BF16).reshape(groups, CAPACITY * q_rows, HEAD_DIM)
    q_res = q_pair[side].reshape(n_rows, HEAD_DIM)
    o, top, norm = all_steps(q_res, ks_res[0], ks_res[1])
    rows3 = (res_rows, q_rows, HEAD_DIM)
    step_part[...] = o.reshape(rows3)
    step_stat[0] = jnp.broadcast_to(top, o.shape).reshape(rows3)
    step_stat[1] = jnp.broadcast_to(norm, o.shape).reshape(rows3)

    blocks = seg // TILE
    scores = prefill(MIDDLE, blocks - 1, next_scores, after=True)
    part_pair.wait()
    stat_pair.wait()
    prefill_rest(blocks - 1, scores)
    out_second = out_rows(MIDDLE, blocks, 1)

    def put_row(dst_row, x):
        for a in range(Q_PER_KV):
            dout[dst_row, :, a * HEAD_DIM:(a + 1) * HEAD_DIM] = x[a * n_step:(a + 1) * n_step].astype(BF16)

    def merge(r, carry):
        top_own, top_step = own_stat[0, side, r], step_stat[0, r]
        top_got = jnp.sum(jnp.where(lane == r, stat_recv[0], 0.0), axis=1, keepdims=True)
        norm_got = jnp.sum(jnp.where(lane == r, stat_recv[1], 0.0), axis=1, keepdims=True)
        joint = jnp.maximum(jnp.maximum(top_own, top_step), top_got)
        w_own = jnp.exp2(top_own - joint)
        w_step = jnp.exp2(top_step - joint)
        w_got = jnp.exp2(top_got - joint)
        norm = own_stat[1, side, r] * w_own + step_stat[1, r] * w_step + norm_got * w_got
        x = own_part[side, r] * w_own + step_part[r] * w_step + part_recv[r].astype(F32) * w_got
        put_row(r, x / norm)
        return carry

    for r in range(res_rows):
        merge(r, 0)
    out_res = pltpu.make_async_copy(
        dout.at[pl.ds(0, res_rows)], dout_hbm.at[pl.ds(0, res_rows)], out_sem.at[2]
    )
    out_res.start()

    def wait_answer(d, carry):
        peer = (me + d) % groups
        pltpu.make_async_remote_copy(
            src_ref=ans_send.at[peer],
            dst_ref=ans_recv.at[peer],
            send_sem=ans_send_sem.at[peer],
            recv_sem=ans_recv_sem.at[peer],
            device_id={"group": peer},
            device_id_type=MESH,
        ).wait()
        return carry

    lax.fori_loop(1, groups, wait_answer, 0)

    def arrive(src, carry):
        count = jnp.int32(0)
        for f in range(finished):
            count = count + jnp.where(owners[src * finished + f] == me, 1, 0)
        for c in range(CAPACITY):
            rows = slice(c * q_rows, (c + 1) * q_rows)
            x = jnp.where(
                count > c, ans_recv[src, rows].astype(F32), step_only[src, rows].astype(F32)
            )
            put_row(res_rows + src * CAPACITY + c, x)
        return carry

    lax.fori_loop(0, groups, arrive, 0, unroll=2)
    arrived = pl.ds(res_rows, groups * CAPACITY)
    out_arr = pltpu.make_async_copy(dout.at[arrived], dout_hbm.at[arrived], out_sem.at[3])
    out_arr.start()
    out_first.wait()
    out_second.wait()
    out_res.wait()
    out_arr.wait()


def per_device(*args):
    q_prefill, kv_fresh, kv_pool, table, lengths, owners, q_decode, kv_steps, kv_res, res_len = args
    groups = lax.axis_size("group")
    rows, n_step, width = q_decode.shape
    res_rows = kv_res.shape[1]
    arr_rows = rows - res_rows
    q_rows = Q_PER_KV * n_step
    seg = q_prefill.shape[0]
    finished = owners.shape[0] // groups
    vmem = pltpu.VMEM
    scratch = [
        vmem(q_prefill.shape, BF16),
        vmem(kv_fresh.shape, BF16),
        vmem(kv_pool.shape, BF16),
        vmem(q_decode.shape, BF16),
        vmem(kv_steps.shape, BF16),
        vmem(kv_res.shape, BF16),
        vmem(q_prefill.shape, BF16),
        vmem(q_decode.shape, BF16),
        vmem((MAXLEN + seg, HEAD_DIM), BF16),
        vmem((MAXLEN + seg, 2 * HEAD_DIM), BF16),
        vmem((STACK * TILE, TILE), F32),
        vmem((max(AHEAD, 1), STACK * TILE, 2 * HEAD_DIM), F32),
        vmem((max(AHEAD, 1), STACK * TILE, HEAD_DIM), F32),
        vmem((2, res_rows, q_rows, HEAD_DIM), BF16),
        vmem((groups, PACK, HEAD_DIM), BF16),
        vmem((groups, PACK, HEAD_DIM), BF16),
        vmem((2, res_rows * n_step, HEAD_DIM), BF16),
        vmem((2, arr_rows * n_step, HEAD_DIM), BF16),
        vmem((res_rows, q_rows, HEAD_DIM), F32),
        vmem((2, res_rows, q_rows, HEAD_DIM), F32),
        vmem((groups, CAPACITY * q_rows, HEAD_DIM), BF16),
        vmem((finished, q_rows, HEAD_DIM), BF16),
        vmem((groups, CAPACITY * q_rows, HEAD_DIM), BF16),
        vmem((groups, CAPACITY * q_rows, HEAD_DIM), BF16),
        vmem((2, res_rows, q_rows, HEAD_DIM), BF16),
        vmem((res_rows, q_rows, HEAD_DIM), BF16),
        vmem((2, q_rows, HEAD_DIM), F32),
        vmem((2, q_rows, HEAD_DIM), F32),
        vmem((2, res_rows, q_rows, HEAD_DIM), F32),
        vmem((2, 2, res_rows, q_rows, HEAD_DIM), F32),
        pltpu.SemaphoreType.DMA((6,)),
        pltpu.SemaphoreType.DMA((4,)),
        pltpu.SemaphoreType.DMA((groups,)),
        pltpu.SemaphoreType.DMA((groups,)),
        pltpu.SemaphoreType.DMA((groups,)),
        pltpu.SemaphoreType.DMA((groups,)),
        pltpu.SemaphoreType.DMA((3,)),
        pltpu.SemaphoreType.DMA((3,)),
    ]
    hbm = pl.BlockSpec(memory_space=pl.ANY)
    smem = pl.BlockSpec(memory_space=pltpu.SMEM)
    return pl.pallas_call(
        functools.partial(kernel, groups),
        out_shape=(
            jax.ShapeDtypeStruct(q_prefill.shape, BF16),
            jax.ShapeDtypeStruct(q_decode.shape, BF16),
        ),
        in_specs=[hbm, hbm, hbm, smem, smem, smem, hbm, hbm, hbm, smem],
        out_specs=(hbm, hbm),
        scratch_shapes=scratch,
        compiler_params=pltpu.CompilerParams(
            collective_id=0, has_side_effects=True, vmem_limit_bytes=56 * 2**20
        ),
        cost_estimate=pl.CostEstimate(
            flops=8 * 10**9, bytes_accessed=21 * 10**6, transcendentals=14 * 10**6
        ),
    )(*args)


def solution(mesh):
    in_specs = (
        P("group", "tp"),
        P(None, "group", "tp"),
        P(None, "group", None, "tp"),
        P("group", None),
        P(),
        P(),
        P("group", None, "tp"),
        P(None, "group", None, "tp"),
        P(None, "group", "tp", None),
        P("group"),
    )
    out_specs = (P("group", "tp"), P("group", None, "tp"))
    return jax.shard_map(
        per_device, mesh=mesh, in_specs=in_specs, out_specs=out_specs, check_vma=False
    )
```
